768 devices in a mesh: lat: 192 (over z, y, core), lev: 4 (over x).
Axes of the slice: x: 4, y: 8, z: 12, core: 2. Of those that a mesh axis runs over, the one named last changes fastest.
Arguments:
- spectral_in: bfloat16 [4, 192, 4, 1280], P('lev', 'lat'), may hold values from -0.25 to 0.25
- legendre: bfloat16 [4, 192, 640, 384], P('lev', 'lat'), may hold values from -0.25 to 0.25
- slot_wave: int32 [4, 192], replicated, may hold values from 0 to 640, as said below
- row_length: int32 [384], P('lat'), may hold values from 16 to 2688, as said below
- quad_weight: float32 [384], replicated, may hold values from 8 to 64
Outputs:
- grid_field: bfloat16 [4, 384, 2688], P('lev', 'lat')
- spectral_out: bfloat16 [4, 192, 4, 1280], P('lev', 'lat')
The draws below stay inside these ranges and needn't reach their ends.
Inputs may be any that keep to these rules, and one draw needn't show every extreme that they name: `slot_wave`: each wavenumber 0 to 639 stands in exactly one slot; all other slots hold 640. Each device holds at most 1 of the wavenumbers. `row_length`: lengths are multiples of 4; the two middle rows have length 2688.
All inputs are finite; a program needn't handle non-finite values.
Results may differ from the reference program's by a relative error of at most 0.0072.
Values may be sent and summed in bfloat16 or wider, within the bound.
No kernel may reach another device: no remote copies, remote signals or barrier semaphores. Data moves between devices by JAX's collectives and lax.ppermute only.
A program may use at most 32 MiB of HBM per device.

```python
import math
import jax
import jax.numpy as jnp
from jax import lax

M = 640
NDEG = 640
NLON = 2688
NLAT = 384
FIELDS = 4
OWN_LAT = 1
OWN = 192
N_LAT = 192
N_LEV = 4


def draw_slot_wave(key, part):
    key = jax.random.fold_in(key, 11)
    first_key, second_key = jax.random.split(key)
    total_slots = N_LEV * OWN
    slot_index = jnp.arange(total_slots, dtype=jnp.int32)
    owner_device = slot_index // OWN * N_LAT + slot_index % OWN // OWN_LAT
    ranks = jax.random.permutation(first_key, total_slots).astype(jnp.int32)
    busiest = jax.random.randint(second_key, (), 0, N_LEV * N_LAT, dtype=jnp.int32)
    scores = ranks - jnp.where(owner_device == busiest, total_slots, 0).astype(jnp.int32)
    ordering = jnp.argsort(scores, stable=True).astype(jnp.int32)
    wave_ids = jnp.full((total_slots,), M, dtype=jnp.int32)
    wave_ids = wave_ids.at[ordering[:M]].set(jnp.arange(M, dtype=jnp.int32))
    return wave_ids.reshape(N_LEV, OWN)


def draw_row_length(key, part):
    key = jax.random.fold_in(key, 23)
    row_index = jnp.arange(NLAT, dtype=jnp.int32)
    distance = jnp.minimum(row_index, NLAT - 1 - row_index)
    half_count = NLAT // 2
    base_length = 16 + 4 * ((NLON - 16) // 4 * (distance + 1) // half_count)
    jitter = 4 * jax.random.randint(key, (NLAT,), 0, 4, dtype=jnp.int32)
    length = jnp.where(distance == half_count - 1, NLON, jnp.maximum(base_length - jitter, 16))
    return length.astype(jnp.int32)


def block_scale(own_key, extent, cuts, smallest, high):
    def one(dim, shards_of):
        heights = jax.random.uniform(jax.random.fold_in(jax.random.fold_in(own_key, 6), dim), (shards_of,), jnp.float32, smallest / len(cuts), high / len(cuts))
        return jnp.repeat(jnp.exp(heights), extent[dim] // shards_of).reshape((-1,) + (1,) * (len(extent) - dim - 1))

    factor_of = one(*cuts[0])
    for cut in cuts[1:]:
        factor_of = factor_of * one(*cut)
    return factor_of


def noise(own_key, dims, width, limit, cuts=(), held_as=jnp.bfloat16):
    loudness = block_scale(own_key, dims, cuts, -0.22, 0.18) if cuts else 1.0
    array = jax.random.normal(own_key, dims, jnp.float32) * width * loudness
    return jnp.minimum(jnp.maximum(array, -limit), limit).astype(held_as)


def setup_inputs(seed: int = 0) -> dict:
    key_of = jax.random.split(jax.random.key(seed), 6)
    return {
        "spectral_in": noise(key_of[0], (N_LEV, OWN, FIELDS, 2 * NDEG), 0.04, 0.25, ((0, 4), (1, 192))),
        "legendre": noise(key_of[1], (N_LEV, OWN, NDEG, NLAT), NDEG ** -0.5, 0.25, ((0, 4), (1, 192))),
        "slot_wave": draw_slot_wave(jax.random.fold_in(key_of[5], 71), 0),
        "row_length": draw_row_length(jax.random.fold_in(key_of[5], 71), 0),
        "quad_weight": jnp.clip(jnp.exp(jax.random.uniform(key_of[4], (NLAT,), jnp.float32, math.log(8.0), math.log(64.0))), 8.0, 64.0),
    }


def transform_row(coeffs_row, length, wave_ids):
    lon_index = jnp.arange(NLON, dtype=jnp.int32)
    phase_turn = (wave_ids[:, None] * lon_index[None, :]) % length
    step_angle = (2.0 * math.pi) / length.astype(jnp.float32)
    angles = phase_turn.astype(jnp.float32) * step_angle
    inside = (lon_index[None, :] < length) & (wave_ids[:, None] < M)
    dft_table = jnp.concatenate([jnp.where(inside, jnp.cos(angles), 0.0), jnp.where(inside, jnp.sin(angles), 0.0)], 0).astype(jnp.bfloat16)
    factor = jnp.where(wave_ids == 0, 1.0, 2.0).astype(jnp.bfloat16)
    stacked = jnp.concatenate([coeffs_row[:, :, 0] * factor[:, None], -(coeffs_row[:, :, 1] * factor[:, None])], 0)
    grid_raw = jnp.dot(stacked.T, dft_table, preferred_element_type=jnp.float32)
    shaped = (grid_raw * (1.0 + 0.5 * jnp.tanh(grid_raw))).astype(jnp.bfloat16)
    summed = jnp.dot(shaped, dft_table.T, preferred_element_type=jnp.float32)
    slot_count = wave_ids.shape[0]
    length_float = length.astype(jnp.float32)
    real_back = summed[:, :slot_count] / length_float
    imag_back = -summed[:, slot_count:] / length_float
    four_row = jnp.stack([real_back, imag_back], -1).astype(jnp.bfloat16)
    return shaped, jnp.transpose(four_row, (1, 0, 2))


def reference(spectral_in, legendre, slot_wave, row_length, quad_weight):
    wave_ids = slot_wave.reshape(-1)
    slot_count = wave_ids.shape[0]
    keep_mask = (jnp.arange(NDEG, dtype=jnp.int32)[None, :] >= wave_ids[:, None]).astype(jnp.bfloat16)
    coeffs = spectral_in.reshape(slot_count, FIELDS, 2, NDEG) * keep_mask[:, None, None, :]
    coeffs = coeffs.reshape(slot_count, FIELDS * 2, NDEG)
    matrices = legendre.reshape(slot_count, NDEG, NLAT)

    def inverse_slot(packed):
        return jnp.dot(packed[0], packed[1], preferred_element_type=jnp.float32).astype(jnp.bfloat16)

    fourier = lax.map(inverse_slot, (coeffs, matrices))
    four_rows = jnp.transpose(fourier.reshape(slot_count, FIELDS, 2, NLAT), (3, 0, 1, 2))

    def one_row(packed):
        return transform_row(packed[0], packed[1], wave_ids)

    shaped_rows, four_out = lax.map(one_row, (four_rows, row_length))
    grid_field = jnp.transpose(shaped_rows, (1, 0, 2))
    weighted = (four_out * quad_weight[:, None, None, None]).astype(jnp.bfloat16)
    weighted = jnp.transpose(weighted.reshape(NLAT, slot_count, FIELDS * 2), (1, 2, 0))

    def direct_slot(packed):
        return jnp.dot(packed[0], packed[1].T, preferred_element_type=jnp.float32)

    direct = lax.map(direct_slot, (weighted, matrices)) * keep_mask[:, None, :].astype(jnp.float32)
    spectral_out = direct.reshape(N_LEV, OWN, FIELDS, 2 * NDEG).astype(jnp.bfloat16)
    return grid_field, spectral_out
```

```python
import math

import jax
import jax.numpy as jnp
from jax import lax
from jax.experimental import pallas as pl
from jax.experimental.pallas import tpu as pltpu
from jax.sharding import Mesh
from jax.sharding import PartitionSpec as P

M = 640
NDEG = 640
NLAT = 384
NLON = 2688
SLOTS = 768
ZC = 24
YX = 32
NB = 128
NA = 21
NA_PAD = 24

F32 = jnp.float32
BF16 = jnp.bfloat16


def iota(shape, dim):
    return lax.broadcasted_iota(jnp.int32, shape, dim)


def dot(x, y, dims=((1,), (0,))):
    return lax.dot_general(x, y, (dims, ((), ())), preferred_element_type=F32)


def one_hot(cond):
    return jnp.where(cond, 1.0, 0.0).astype(BF16)


def row_selector():
    l = iota((NLAT, 128), 0)
    return one_hot((((l >> 2) & 7) * 2 + (l & 1)) == (iota((NLAT, 128), 1) & 15))


def row_target():
    l = iota((ZC, NLAT), 1)
    return ((l >> 5) * 2 + ((l >> 1) & 1)) == iota((ZC, NLAT), 0)


def pair_selector():
    p = iota((128, 128), 0)
    target = ((p >> 6) * 4 + (p & 3)) * 16 + ((p >> 2) & 7) * 2 + ((p >> 5) & 1)
    return one_hot(iota((128, 128), 1) == target)


def by24(l):
    return (l * 2731) >> 16


def slot_selector():
    l = iota((128, SLOTS), 1)
    return one_hot((iota((128, SLOTS), 0) & 31) == (l - by24(l) * ZC))


def legendre_in(spec, leg, wave):
    both = jnp.concatenate([spec[:, :NDEG].astype(F32), spec[:, NDEG:].astype(F32)], 0)
    kept = jnp.where(iota(both.shape, 1) >= wave, both, 0.0).astype(BF16)
    four = dot(kept, leg).astype(BF16).astype(F32)
    mine = row_target()
    spread = jnp.concatenate([jnp.where(mine, four[q : q + 1], 0.0) for q in range(8)], 0)
    moved = dot(spread.astype(BF16), row_selector())
    group = iota((ZC, 128), 1) >> 4
    out = jnp.zeros((ZC, 128), F32)
    for q in range(8):
        out = jnp.where(group == q, moved[q * ZC : (q + 1) * ZC], out)
    return out


def turn_in(got):
    padded = jnp.concatenate([got, jnp.zeros((32 - ZC, 128), F32)], 0)
    moved = dot(pair_selector(), jnp.concatenate([padded] * 4, 0).astype(BF16), ((1,), (1,)))
    group = iota((YX, 128), 1) >> 5
    out = jnp.zeros((YX, 128), F32)
    for q in range(4):
        out = jnp.where(group == q, moved[q * YX : (q + 1) * YX], out)
    return out


def spread_groups(x, count, width):
    group = iota(x.shape, 1) >> width
    return jnp.concatenate([jnp.where(group == q, x, 0.0) for q in range(count)], 0).astype(BF16)


def turn_out(got):
    moved = dot(spread_groups(got, 4, 5), pair_selector(), ((0,), (0,)))
    total = moved[:32] + moved[32:64] + moved[64:96] + moved[96:]
    return total[:ZC]


def legendre_out(got, leg, wave):
    moved = dot(spread_groups(got, 8, 4), row_selector(), ((1,), (1,)))
    mine = row_target()
    rows = [
        jnp.sum(jnp.where(mine, moved[q * ZC : (q + 1) * ZC], 0.0), 0, keepdims=True)
        for q in range(8)
    ]
    weighted = jnp.concatenate(rows, 0).astype(BF16)
    result = dot(weighted, leg, ((1,), (1,)))
    result = jnp.where(iota(result.shape, 1) >= wave, result, 0.0)
    return result[:4], result[4:]


def slot_order(waves):
    l = iota((192, SLOTS), 1)
    i = by24(l)
    j = l - i * ZC
    pick = one_hot(iota((192, SLOTS), 0) == (((j >> 1) * 8 + (i >> 2)) * 2 + (j & 1)))
    parts = jnp.concatenate([(waves >> 3).astype(F32), (waves & 7).astype(F32)], 0).astype(BF16)
    got = dot(parts, pick)
    full = got[:4] * 8.0 + got[4:]
    lane = iota((4, SLOTS), 1)
    return jnp.sum(jnp.where((by24(lane) & 3) == iota((4, SLOTS), 0), full, 0.0), 0, keepdims=True)


SIN_TERMS = [(-1.0) ** n * math.pi ** (2 * n + 1) / math.factorial(2 * n + 1) for n in range(7)]
COS_TERMS = [(-1.0) ** n * math.pi ** (2 * n) / math.factorial(2 * n) for n in range(8)]


def circle(points, waves, length):
    product = points * waves
    inverse = 1.0 / length
    rest = product - jnp.floor(product * inverse + 0.5) * length
    turn = rest * inverse
    square = turn * turn
    sine = jnp.full_like(square, SIN_TERMS[-1])
    for term in SIN_TERMS[-2::-1]:
        sine = sine * square + term
    sine = sine * turn
    cosine = jnp.full_like(square, COS_TERMS[-1])
    for term in COS_TERMS[-2::-1]:
        cosine = cosine * square + term
    return 1.0 - 2.0 * sine * sine, 2.0 * sine * cosine


def split(x):
    high = x.astype(BF16)
    return high, (x - high.astype(F32)).astype(BF16)


def table_a(waves, length):
    points = iota((NA_PAD, SLOTS), 0).astype(F32) * float(NB)
    cosine, sine = circle(points, waves, length)
    both = jnp.concatenate([cosine, sine], 1)
    high, low = split(both)
    return jnp.concatenate([high.astype(F32), low.astype(F32)], 0).astype(BF16)


def table_b(waves, length):
    return circle(iota((NB, waves.shape[1]), 0).astype(F32), waves, length)


def gather_slots(got):
    moved = dot(spread_groups(got, 4, 5), slot_selector())
    own = by24(iota((YX, SLOTS), 1)) == iota((YX, SLOTS), 0)
    return [
        jnp.sum(jnp.where(own, moved[q * YX : (q + 1) * YX], 0.0), 0, keepdims=True)
        for q in range(4)
    ]


def grid_row(real, imag, waves, length, weight, outer, cosine, sine):
    factor = jnp.where(waves >= float(M), 0.0, jnp.where(waves == 0.0, 1.0, 2.0))
    real = real * factor
    imag = imag * factor
    mixed = jnp.concatenate([real * cosine - imag * sine, -(real * sine + imag * cosine)], 1)
    high, low = split(mixed)
    raw = dot(outer, high, ((1,), (1,)))
    raw = raw[:NA_PAD] + raw[NA_PAD:] + dot(outer[:NA_PAD], low, ((1,), (1,)))
    shaped = raw * (1.0 + 0.5 * jnp.tanh(raw))
    point = iota((NA_PAD, NB), 0) * NB + iota((NA_PAD, NB), 1)
    shaped = jnp.where(point.astype(F32) < length, shaped, 0.0)
    rounded = shaped.astype(BF16).astype(F32)
    twice = jnp.concatenate([rounded, rounded], 0).astype(BF16)
    back = dot(twice, outer, ((0,), (0,)))
    back_cos, back_sin = back[:, :SLOTS], back[:, SLOTS:]
    live = jnp.where(waves >= float(M), 0.0, 1.0) / length
    out_real = jnp.sum(back_cos * cosine - back_sin * sine, 0, keepdims=True) * live
    out_imag = -jnp.sum(back_cos * sine + back_sin * cosine, 0, keepdims=True) * live
    out = [(v.astype(BF16).astype(F32) * weight).astype(BF16).astype(F32) for v in (out_real, out_imag)]
    return rounded, out[0], out[1]


def scatter_slots(rows):
    own = by24(iota((YX, SLOTS), 1)) == iota((YX, SLOTS), 0)
    spread = jnp.concatenate([jnp.where(own, row, 0.0) for row in rows], 0).astype(BF16)
    moved = dot(spread, slot_selector(), ((1,), (1,)))
    group = iota((YX, 128), 1) >> 5
    out = jnp.zeros((YX, 128), F32)
    for q in range(4):
        out = jnp.where(group == q, moved[q * YX : (q + 1) * YX], out)
    return out


def my_wave(place_ref, waves_ref):
    return waves_ref[place_ref[0], place_ref[1]]


def legendre_in_kernel(place_ref, waves_ref, spec_ref, leg_ref, out_ref):
    out = legendre_in(spec_ref[0, 0], leg_ref[0, 0], my_wave(place_ref, waves_ref))
    out_ref[...] = out.reshape(ZC, 1, 128)


def turn_in_kernel(got_ref, out_ref):
    out_ref[...] = turn_in(got_ref[...].reshape(ZC, 128)).reshape(YX, 1, 128)


def tables_kernel(length_ref, waves_ref, order_ref, outer_ref, cos_ref, sin_ref):
    waves = slot_order(waves_ref[...])
    order_ref[...] = waves
    for r in range(2):
        length = length_ref[r].astype(F32)
        outer_ref[r] = table_a(waves, length)
        for part in range(SLOTS // 128):
            lanes = slice(part * 128, (part + 1) * 128)
            cosine, sine = table_b(waves[:, lanes], length)
            cos_ref[r, :, lanes] = cosine
            sin_ref[r, :, lanes] = sine


def grid_kernel(
    place_ref, length_ref, weight_ref, got_ref, order_ref, outer_ref, cos_ref, sin_ref, grid_ref, out_ref
):
    rows = gather_slots(got_ref[...].reshape(YX, 128))
    done = []
    for r in range(2):
        done.append(
            grid_row(
                rows[r],
                rows[2 + r],
                order_ref[...],
                length_ref[r].astype(F32),
                weight_ref[2 * place_ref[1] + r],
                outer_ref[r],
                cos_ref[r],
                sin_ref[r],
            )
        )
    for a in range(NA):
        pair = jnp.concatenate([done[0][0][a : a + 1], done[1][0][a : a + 1]], 0)
        grid_ref[0, :, a * NB : (a + 1) * NB] = pair.astype(BF16)
    out = scatter_slots([done[0][1], done[1][1], done[0][2], done[1][2]])
    out_ref[...] = out.reshape(YX, 1, 128)


def turn_out_kernel(got_ref, out_ref):
    out_ref[...] = turn_out(got_ref[...].reshape(YX, 128)).reshape(ZC, 1, 128)


def legendre_out_kernel(place_ref, waves_ref, got_ref, leg_ref, out_ref):
    real, imag = legendre_out(
        got_ref[...].reshape(ZC, 128), leg_ref[0, 0], my_wave(place_ref, waves_ref)
    )
    out_ref[0, 0, :, :NDEG] = real.astype(BF16)
    out_ref[0, 0, :, NDEG:] = imag.astype(BF16)


VMEM = pl.BlockSpec(memory_space=pltpu.VMEM)
SMEM = pl.BlockSpec(memory_space=pltpu.SMEM)


def call(kernel, name, in_specs, outs, cost):
    single = not isinstance(outs, list)
    return pl.pallas_call(
        kernel,
        name=name,
        in_specs=in_specs,
        out_specs=VMEM if single else [VMEM] * len(outs),
        out_shape=outs if single else tuple(outs),
        compiler_params=pltpu.CompilerParams(vmem_limit_bytes=24 * 1024 * 1024),
        cost_estimate=pl.CostEstimate(flops=cost, bytes_accessed=100000, transcendentals=0),
    )


def shape(*dims, dtype=F32):
    return jax.ShapeDtypeStruct(dims, dtype)


def shards(spectral_in, legendre, slot_wave, row_length, quad_weight):
    lat_index = (lax.axis_index("z") * 8 + lax.axis_index("y")) * 2 + lax.axis_index("c")
    place = jnp.stack([lax.axis_index("x"), lat_index]).astype(jnp.int32)
    to_send = call(legendre_in_kernel, "legendre_in", [SMEM, SMEM, VMEM, VMEM], shape(ZC, 1, 128), 10**6)(
        place, slot_wave, spectral_in, legendre
    )
    got = lax.all_to_all(to_send, ("z", "c"), 0, 0, tiled=True)
    to_send = call(turn_in_kernel, "turn_in", [VMEM], shape(YX, 1, 128), 10**6)(got)
    got = lax.all_to_all(to_send, ("y", "x"), 0, 0, tiled=True)
    order, outer, cosine, sine = call(
        tables_kernel,
        "tables",
        [SMEM, VMEM],
        [
            shape(1, SLOTS),
            shape(2, 2 * NA_PAD, 2 * SLOTS, dtype=BF16),
            shape(2, NB, SLOTS),
            shape(2, NB, SLOTS),
        ],
        10**9,
    )(row_length, slot_wave)
    grid_field, to_send = call(
        grid_kernel,
        "grid",
        [SMEM, SMEM, SMEM, VMEM, VMEM, VMEM, VMEM, VMEM],
        [shape(1, 2, NLON, dtype=BF16), shape(YX, 1, 128)],
        10**6,
    )(place, row_length, quad_weight, got, order, outer, cosine, sine)
    got = lax.all_to_all(to_send, ("y", "x"), 0, 0, tiled=True)
    to_send = call(turn_out_kernel, "turn_out", [VMEM], shape(ZC, 1, 128), 10**6)(got)
    got = lax.all_to_all(to_send, ("z", "c"), 0, 0, tiled=True)
    spectral_out = call(
        legendre_out_kernel, "legendre_out", [SMEM, SMEM, VMEM, VMEM], shape(1, 1, 4, 2 * NDEG, dtype=BF16), 10**6
    )(place, slot_wave, got, legendre)
    return grid_field, spectral_out


def solution(mesh):
    cut = Mesh(mesh.devices.reshape(12, 8, 2, 4), ("z", "y", "c", "x"))
    lat = ("z", "y", "c")
    in_specs = (P("x", lat, None, None), P("x", lat, None, None), P(), P(lat), P())
    out_specs = (P("x", lat, None), P("x", lat, None, None))
    return jax.shard_map(shards, mesh=cut, in_specs=in_specs, out_specs=out_specs, check_vma=False)
```

```python
import math

import jax
import jax.numpy as jnp
from jax import lax
from jax.experimental import pallas as pl
from jax.experimental.pallas import tpu as pltpu
from jax.sharding import Mesh
from jax.sharding import PartitionSpec as P

M = 640
NDEG = 640
NLAT = 384
NLON = 2688
SLOTS = 768
ZC = 24
YX = 32
NB = 128
NA = 21
NA_PAD = 24

F32 = jnp.float32
BF16 = jnp.bfloat16


def iota(shape, dim):
    return lax.broadcasted_iota(jnp.int32, shape, dim)


def dot(x, y, dims=((1,), (0,))):
    return lax.dot_general(x, y, (dims, ((), ())), preferred_element_type=F32)


def one_hot(cond):
    return jnp.where(cond, 1.0, 0.0).astype(BF16)


def row_selector():
    l = iota((NLAT, 128), 0)
    return one_hot((((l >> 2) & 7) * 2 + (l & 1)) == (iota((NLAT, 128), 1) & 15))


def row_target():
    l = iota((ZC, NLAT), 1)
    return ((l >> 5) * 2 + ((l >> 1) & 1)) == iota((ZC, NLAT), 0)


def pair_selector():
    p = iota((128, 128), 0)
    target = ((p >> 6) * 4 + (p & 3)) * 16 + ((p >> 2) & 7) * 2 + ((p >> 5) & 1)
    return one_hot(iota((128, 128), 1) == target)


def by24(l):
    return (l * 2731) >> 16


def slot_selector():
    l = iota((128, SLOTS), 1)
    return one_hot((iota((128, SLOTS), 0) & 31) == (l - by24(l) * ZC))


def legendre_in(spec, leg, wave):
    both = jnp.concatenate([spec[:, :NDEG].astype(F32), spec[:, NDEG:].astype(F32)], 0)
    kept = jnp.where(iota(both.shape, 1) >= wave, both, 0.0).astype(BF16)
    four = dot(kept, leg).astype(BF16).astype(F32)
    mine = row_target()
    spread = jnp.concatenate([jnp.where(mine, four[q : q + 1], 0.0) for q in range(8)], 0)
    moved = dot(spread.astype(BF16), row_selector())
    group = iota((ZC, 128), 1) >> 4
    out = jnp.zeros((ZC, 128), F32)
    for q in range(8):
        out = jnp.where(group == q, moved[q * ZC : (q + 1) * ZC], out)
    return out


def turn_in(got):
    padded = jnp.concatenate([got, jnp.zeros((32 - ZC, 128), F32)], 0)
    moved = dot(pair_selector(), jnp.concatenate([padded] * 4, 0).astype(BF16), ((1,), (1,)))
    group = iota((YX, 128), 1) >> 5
    out = jnp.zeros((YX, 128), F32)
    for q in range(4):
        out = jnp.where(group == q, moved[q * YX : (q + 1) * YX], out)
    return out


def spread_groups(x, count, width):
    group = iota(x.shape, 1) >> width
    return jnp.concatenate([jnp.where(group == q, x, 0.0) for q in range(count)], 0).astype(BF16)


def turn_out(got):
    moved = dot(spread_groups(got, 4, 5), pair_selector(), ((0,), (0,)))
    total = moved[:32] + moved[32:64] + moved[64:96] + moved[96:]
    return total[:ZC]


def legendre_out(got, leg, wave):
    moved = dot(spread_groups(got, 8, 4), row_selector(), ((1,), (1,)))
    mine = row_target()
    rows = [
        jnp.sum(jnp.where(mine, moved[q * ZC : (q + 1) * ZC], 0.0), 0, keepdims=True)
        for q in range(8)
    ]
    weighted = jnp.concatenate(rows, 0).astype(BF16)
    result = dot(weighted, leg, ((1,), (1,)))
    result = jnp.where(iota(result.shape, 1) >= wave, result, 0.0)
    return result[:4], result[4:]


def slot_order(waves):
    l = iota((192, SLOTS), 1)
    i = by24(l)
    j = l - i * ZC
    pick = one_hot(iota((192, SLOTS), 0) == (((j >> 1) * 8 + (i >> 2)) * 2 + (j & 1)))
    parts = jnp.concatenate([(waves >> 3).astype(F32), (waves & 7).astype(F32)], 0).astype(BF16)
    got = dot(parts, pick)
    full = got[:4] * 8.0 + got[4:]
    lane = iota((4, SLOTS), 1)
    return jnp.sum(jnp.where((by24(lane) & 3) == iota((4, SLOTS), 0), full, 0.0), 0, keepdims=True)


SIN_TERMS = [(-1.0) ** n * math.pi ** (2 * n + 1) / math.factorial(2 * n + 1) for n in range(7)]
COS_TERMS = [(-1.0) ** n * math.pi ** (2 * n) / math.factorial(2 * n) for n in range(8)]


def circle(points, waves, length):
    product = points * waves
    inverse = 1.0 / length
    rest = product - jnp.floor(product * inverse + 0.5) * length
    turn = rest * inverse
    square = turn * turn
    sine = jnp.full_like(square, SIN_TERMS[-1])
    for term in SIN_TERMS[-2::-1]:
        sine = sine * square + term
    sine = sine * turn
    cosine = jnp.full_like(square, COS_TERMS[-1])
    for term in COS_TERMS[-2::-1]:
        cosine = cosine * square + term
    return 1.0 - 2.0 * sine * sine, 2.0 * sine * cosine


def split(x):
    high = x.astype(BF16)
    return high, (x - high.astype(F32)).astype(BF16)


def tables(waves, length):
    row = iota((48, SLOTS), 0)
    points = jnp.where(row < NA_PAD, row * NB, jnp.where(row < 40, (row - NA_PAD) * 8, row - 40))
    cosine, sine = circle(points.astype(F32), waves, length)
    high, low = split(jnp.concatenate([cosine[:NA_PAD], sine[:NA_PAD]], 1))
    outer = jnp.concatenate([high.astype(F32), low.astype(F32)], 0).astype(BF16)
    return outer, cosine[NA_PAD:], sine[NA_PAD:]


def gather_slots(got):
    moved = dot(spread_groups(got, 4, 5), slot_selector())
    own = by24(iota((YX, SLOTS), 1)) == iota((YX, SLOTS), 0)
    return [
        jnp.sum(jnp.where(own, moved[q * YX : (q + 1) * YX], 0.0), 0, keepdims=True)
        for q in range(4)
    ]


def factors(waves, lengths, weights):
    empty = waves >= float(M)
    rows = [jnp.where(empty, 0.0, jnp.where(waves == 0.0, 1.0, 2.0))]
    rows += [jnp.where(empty, 0.0, w / n) for n, w in zip(lengths, weights, strict=True)]
    rows += [jnp.full_like(waves, n) for n in lengths]
    return jnp.concatenate(rows + [jnp.zeros((3, SLOTS), F32)], 0)


def grid_row(real, imag, factor, back_factor, length, outer, cosine, sine):
    real = real * factor
    imag = imag * factor
    cos_one, sin_one = cosine[16:], sine[16:]
    start_real = real * cos_one - imag * sin_one
    start_imag = real * sin_one + imag * cos_one
    mixed = []
    for j in range(16):
        c, s = cosine[j : j + 1], sine[j : j + 1]
        mixed.append(
            jnp.concatenate([start_real * c - start_imag * s, -(start_real * s + start_imag * c)], 1)
        )
    high, low = split(jnp.concatenate(mixed, 0))
    raw = dot(outer, high, ((1,), (1,)))
    raw = raw[:NA_PAD] + raw[NA_PAD:] + dot(outer[:NA_PAD], low, ((1,), (1,)))
    shaped = raw * (1.0 + 0.5 * jnp.tanh(raw))
    point = iota((NA_PAD, NB), 0) * NB + iota((NA_PAD, NB), 1)
    shaped = jnp.where(point.astype(F32) < length[:, :NB], shaped, 0.0)
    rounded = shaped.astype(BF16).astype(F32)
    twice = jnp.concatenate([rounded, rounded], 0).astype(BF16)
    back = dot(twice, outer, ((0,), (0,)))
    total_cos = jnp.zeros((8, SLOTS), F32)
    total_sin = jnp.zeros((8, SLOTS), F32)
    for j in range(16):
        c, s = cosine[j : j + 1], sine[j : j + 1]
        rows = slice(j * 8, (j + 1) * 8)
        back_cos, back_sin = back[rows, :SLOTS], back[rows, SLOTS:]
        total_cos = total_cos + (back_cos * c - back_sin * s)
        total_sin = total_sin + (back_cos * s + back_sin * c)
    out_real = jnp.sum(total_cos * cos_one - total_sin * sin_one, 0, keepdims=True)
    out_imag = -jnp.sum(total_cos * sin_one + total_sin * cos_one, 0, keepdims=True)
    return rounded, out_real * back_factor, out_imag * back_factor


def scatter_slots(rows):
    own = by24(iota((YX, SLOTS), 1)) == iota((YX, SLOTS), 0)
    spread = jnp.concatenate([jnp.where(own, row, 0.0) for row in rows], 0).astype(BF16)
    moved = dot(spread, slot_selector(), ((1,), (1,)))
    group = iota((YX, 128), 1) >> 5
    out = jnp.zeros((YX, 128), F32)
    for q in range(4):
        out = jnp.where(group == q, moved[q * YX : (q + 1) * YX], out)
    return out


def tables_kernel(
    place_ref, waves_ref, length_ref, weight_ref, wave_ref, factor_ref, outer_ref, cos_ref, sin_ref
):
    waves = waves_ref[...]
    here = (iota((4, 192), 0) == place_ref[0]) & (iota((4, 192), 1) == place_ref[1])
    own = jnp.where(here, waves.astype(F32), 0.0)
    own = jnp.sum(jnp.sum(own, 0, keepdims=True), 1, keepdims=True)
    wave_ref[...] = jnp.broadcast_to(own, (1, 128))
    order = slot_order(waves)
    lengths = [length_ref[r].astype(F32) for r in range(2)]
    factor_ref[...] = factors(order, lengths, [weight_ref[2 * place_ref[1] + r] for r in range(2)])
    for r in range(2):
        outer_ref[r], cos_ref[r], sin_ref[r] = tables(order, lengths[r])


def legendre_in_kernel(wave_ref, spec_ref, leg_ref, out_ref):
    wave = wave_ref[:, :1].astype(jnp.int32)
    out_ref[...] = legendre_in(spec_ref[0, 0], leg_ref[0, 0], wave).reshape(ZC, 1, 128)


def turn_in_kernel(got_ref, out_ref):
    out_ref[...] = turn_in(got_ref[...].reshape(ZC, 128)).reshape(YX, 1, 128)


def grid_kernel(got_ref, factor_ref, outer_ref, cos_ref, sin_ref, grid_ref, out_ref):
    rows = gather_slots(got_ref[...].reshape(YX, 128))
    done = []
    for r in range(2):
        done.append(
            grid_row(
                rows[r],
                rows[2 + r],
                factor_ref[0:1],
                factor_ref[1 + r : 2 + r],
                factor_ref[3 + r : 4 + r],
                outer_ref[r],
                cos_ref[r],
                sin_ref[r],
            )
        )
    for a in range(NA):
        pair = jnp.concatenate([done[0][0][a : a + 1], done[1][0][a : a + 1]], 0)
        grid_ref[0, :, a * NB : (a + 1) * NB] = pair.astype(BF16)
    out = scatter_slots([done[0][1], done[1][1], done[0][2], done[1][2]])
    out_ref[...] = out.reshape(YX, 1, 128)


def turn_out_kernel(got_ref, out_ref):
    out_ref[...] = turn_out(got_ref[...].reshape(YX, 128)).reshape(ZC, 1, 128)


def legendre_out_kernel(wave_ref, got_ref, leg_ref, out_ref):
    wave = wave_ref[:, :1].astype(jnp.int32)
    real, imag = legendre_out(got_ref[...].reshape(ZC, 128), leg_ref[0, 0], wave)
    out_ref[0, 0, :, :NDEG] = real.astype(BF16)
    out_ref[0, 0, :, NDEG:] = imag.astype(BF16)


VMEM = pl.BlockSpec(memory_space=pltpu.VMEM)
SMEM = pl.BlockSpec(memory_space=pltpu.SMEM)


def call(kernel, name, in_specs, outs, flops=10**6):
    single = not isinstance(outs, list)
    return pl.pallas_call(
        kernel,
        name=name,
        in_specs=in_specs,
        out_specs=VMEM if single else [VMEM] * len(outs),
        out_shape=outs if single else tuple(outs),
        compiler_params=pltpu.CompilerParams(vmem_limit_bytes=24 * 1024 * 1024),
        cost_estimate=pl.CostEstimate(flops=flops, bytes_accessed=100000, transcendentals=0),
    )


def shape(*dims, dtype=F32):
    return jax.ShapeDtypeStruct(dims, dtype)


def shards(spectral_in, legendre, slot_wave, row_length, quad_weight):
    lat_index = (lax.axis_index("z") * 8 + lax.axis_index("y")) * 2 + lax.axis_index("c")
    place = jnp.stack([lax.axis_index("x"), lat_index]).astype(jnp.int32)
    wave, factor, outer, cosine, sine = call(
        tables_kernel,
        "tables",
        [SMEM, VMEM, SMEM, SMEM],
        [
            shape(1, 128),
            shape(8, SLOTS),
            shape(2, 2 * NA_PAD, 2 * SLOTS, dtype=BF16),
            shape(2, 24, SLOTS),
            shape(2, 24, SLOTS),
        ],
        2 * 10**9,
    )(place, slot_wave, row_length, quad_weight)
    to_send = call(legendre_in_kernel, "legendre_in", [VMEM] * 3, shape(ZC, 1, 128))(
        wave, spectral_in, legendre
    )
    got = lax.all_to_all(to_send, ("z", "c"), 0, 0, tiled=True)
    to_send = call(turn_in_kernel, "turn_in", [VMEM], shape(YX, 1, 128))(got)
    got = lax.all_to_all(to_send, ("y", "x"), 0, 0, tiled=True)
    grid_field, to_send = call(
        grid_kernel, "grid", [VMEM] * 5, [shape(1, 2, NLON, dtype=BF16), shape(YX, 1, 128)]
    )(got, factor, outer, cosine, sine)
    got = lax.all_to_all(to_send, ("y", "x"), 0, 0, tiled=True)
    to_send = call(turn_out_kernel, "turn_out", [VMEM], shape(ZC, 1, 128))(got)
    got = lax.all_to_all(to_send, ("z", "c"), 0, 0, tiled=True)
    spectral_out = call(
        legendre_out_kernel, "legendre_out", [VMEM] * 3, shape(1, 1, 4, 2 * NDEG, dtype=BF16)
    )(wave, got, legendre)
    return grid_field, spectral_out


def solution(mesh):
    cut = Mesh(mesh.devices.reshape(12, 8, 2, 4), ("z", "y", "c", "x"))
    lat = ("z", "y", "c")
    in_specs = (P("x", lat, None, None), P("x", lat, None, None), P(), P(lat), P())
    out_specs = (P("x", lat, None), P("x", lat, None, None))
    return jax.shard_map(shards, mesh=cut, in_specs=in_specs, out_specs=out_specs, check_vma=False)
```

```python
import math

import jax
import jax.numpy as jnp
from jax import lax
from jax.experimental import pallas as pl
from jax.experimental.pallas import tpu as pltpu
from jax.sharding import Mesh
from jax.sharding import PartitionSpec as P

M = 640
NDEG = 640
NLAT = 384
NLON = 2688
SLOTS = 768
ZC = 24
YX = 32
NB = 128
NA = 21
NA_PAD = 24
NT = 48

PARTS = [slice(q * 128, (q + 1) * 128) for q in range(6)]

F32 = jnp.float32
BF16 = jnp.bfloat16


def iota(shape, dim):
    return lax.broadcasted_iota(jnp.int32, shape, dim)


def dot(x, y, dims=((1,), (0,))):
    return lax.dot_general(x, y, (dims, ((), ())), preferred_element_type=F32)


def one_hot(cond):
    return jnp.where(cond, 1.0, 0.0).astype(BF16)


def row_selector():
    l = iota((NLAT, 128), 0)
    lane = iota((NLAT, 128), 1)
    return one_hot((lane & 63) == ((l & 1) * 32 + (l >> 5) * 2 + ((l >> 1) & 1)))


def legendre_in(spec, leg, wave):
    both = jnp.concatenate([spec[:, :NDEG].astype(F32), spec[:, NDEG:].astype(F32)], 0)
    kept = jnp.where(iota(both.shape, 1) >= wave, both, 0.0).astype(BF16)
    four = dot(kept, leg).astype(BF16).astype(F32)
    mine = ((iota((8, NLAT), 1) >> 2) & 7) == iota((8, NLAT), 0)
    spread = jnp.concatenate([jnp.where(mine, four[q : q + 1], 0.0) for q in range(8)], 0)
    moved = dot(spread.astype(BF16), row_selector())
    return jnp.where(iota((YX, 128), 1) < 64, moved[:YX], moved[YX:])


def legendre_out(got, weight, leg, wave):
    low = iota((YX, 128), 1) < 64
    spread = jnp.concatenate([jnp.where(low, got, 0.0), jnp.where(low, 0.0, got)], 0)
    moved = dot(spread.astype(BF16), row_selector(), ((1,), (1,)))
    mine = ((iota((8, NLAT), 1) >> 2) & 7) == iota((8, NLAT), 0)
    rows = [
        jnp.sum(jnp.where(mine, moved[q * 8 : (q + 1) * 8], 0.0), 0, keepdims=True) for q in range(8)
    ]
    weighted = (jnp.concatenate(rows, 0) * weight).astype(BF16)
    result = dot(weighted, leg, ((1,), (1,)))
    result = jnp.where(iota(result.shape, 1) >= wave, result, 0.0)
    return result[:4], result[4:]


def turn(got):
    flipped = jnp.concatenate([got] * 4, 0).T
    group = iota((32, 128), 1) >> 5
    out = flipped[:32]
    for q in range(1, 4):
        out = jnp.where(group == q, flipped[q * 32 : (q + 1) * 32], out)
    return out


def roll(x, shift, axis):
    return pltpu.roll(x, shift % x.shape[axis], axis)


def swap_fours(x):
    line = iota(x.shape, 0) & 3
    group = iota(x.shape, 1) >> 5
    out = x
    for d in range(1, 4):
        moved = roll(x, -32 * d, 1)
        out = jnp.where(line - group == d, roll(moved, d, 0), out)
        out = jnp.where(line - group == d - 4, roll(moved, d - 4, 0), out)
    return out


def slot_order(waves):
    k = iota((192, 128), 0) & 31
    lane = iota((192, 128), 1)
    pick = one_hot(k == ((lane >> 6) * 16 + (lane & 7) * 2 + ((lane >> 5) & 1)))
    both = jnp.concatenate([(waves >> 3).astype(F32), (waves & 7).astype(F32)], 0)
    part = iota((8, 192), 1) >> 5
    spread = jnp.concatenate([jnp.where(part == q, both, 0.0) for q in range(6)], 0)
    moved = dot(spread.astype(BF16), pick)
    row = iota((8, 128), 0)
    scale = jnp.where((row & 3) == ((iota((8, 128), 1) >> 3) & 3), jnp.where(row < 4, 8.0, 1.0), 0.0)
    return jnp.concatenate(
        [jnp.sum(moved[q * 8 : (q + 1) * 8] * scale, 0, keepdims=True) for q in range(6)], 1
    )


SIN_TERMS = [(-1.0) ** n * math.pi ** (2 * n + 1) / math.factorial(2 * n + 1) for n in range(7)]
COS_TERMS = [(-1.0) ** n * math.pi ** (2 * n) / math.factorial(2 * n) for n in range(8)]


def circle(points, waves, length):
    product = points * waves
    inverse = 1.0 / length
    rest = product - jnp.floor(product * inverse + 0.5) * length
    turn = rest * inverse
    square = turn * turn
    sine = jnp.full_like(square, SIN_TERMS[-1])
    for term in SIN_TERMS[-2::-1]:
        sine = sine * square + term
    sine = sine * turn
    cosine = jnp.full_like(square, COS_TERMS[-1])
    for term in COS_TERMS[-2::-1]:
        cosine = cosine * square + term
    return 1.0 - 2.0 * sine * sine, 2.0 * sine * cosine


def split(x):
    high = x.astype(BF16)
    return high, (x - high.astype(F32)).astype(BF16)


def tables(waves, length):
    row = iota((48, SLOTS), 0)
    points = jnp.where(row < NA_PAD, row * NB, jnp.where(row < 40, (row - NA_PAD) * 8, row - 40))
    cosine, sine = circle(points.astype(F32), waves, length)
    parts = []
    for lanes in PARTS:
        parts += [cosine[:NA_PAD, lanes], sine[:NA_PAD, lanes]]
    high, low = split(jnp.concatenate(parts, 1))
    outer = jnp.concatenate([high.astype(F32), low.astype(F32)], 0).astype(BF16)
    return outer, cosine[NA_PAD:], sine[NA_PAD:]


def factors(waves, lengths):
    empty = waves >= float(M)
    rows = [jnp.where(empty, 0.0, jnp.where(waves == 0.0, 1.0, 2.0))]
    rows += [jnp.where(empty, 0.0, 1.0 / n) for n in lengths]
    rows += [jnp.full_like(waves, n) for n in lengths]
    return jnp.concatenate(rows + [jnp.zeros((3, SLOTS), F32)], 0)


def grid_rows(got, factor, outer, cosine, sine):
    got = swap_fours(got)
    raws = [jnp.zeros((NB, NT), F32) for _ in range(2)]
    for q, lanes in enumerate(PARTS):
        for r in range(2):
            wide = slice(q * 256, (q + 1) * 256)
            cos_one, sin_one = cosine[r, 16:, lanes], sine[r, 16:, lanes]
            real = got[q * 4 + r : q * 4 + r + 1] * factor[0:1, lanes]
            imag = got[q * 4 + 2 + r : q * 4 + 3 + r] * factor[0:1, lanes]
            start_real = real * cos_one - imag * sin_one
            start_imag = real * sin_one + imag * cos_one
            mixed = []
            for j in range(16):
                c, s = cosine[r, j : j + 1, lanes], sine[r, j : j + 1, lanes]
                mixed.append(
                    jnp.concatenate([start_real * c - start_imag * s, -(start_real * s + start_imag * c)], 1)
                )
            high = jnp.concatenate(mixed, 0).astype(BF16)
            raws[r] = raws[r] + dot(high, outer[r, :, wide], ((1,), (1,)))
    grids, flips = [], []
    for r in range(2):
        raw = raws[r].T
        raw = raw[:NA_PAD] + raw[NA_PAD:]
        shaped = raw * (1.0 + 0.5 * jnp.tanh(raw))
        point = iota((NA_PAD, NB), 0) * NB + iota((NA_PAD, NB), 1)
        shaped = jnp.where(point.astype(F32) < factor[3 + r : 4 + r, :NB], shaped, 0.0)
        rounded = shaped.astype(BF16).astype(F32)
        grids.append(rounded)
        flips.append(jnp.concatenate([rounded, rounded], 0).T.astype(BF16))
    lines = [None] * 24
    for q, lanes in enumerate(PARTS):
        for r in range(2):
            wide = slice(q * 256, (q + 1) * 256)
            back = dot(flips[r], outer[r, :, wide])
            total_cos = jnp.zeros((8, 128), F32)
            total_sin = jnp.zeros((8, 128), F32)
            for j in range(16):
                c, s = cosine[r, j : j + 1, lanes], sine[r, j : j + 1, lanes]
                rows = slice(j * 8, (j + 1) * 8)
                back_cos, back_sin = back[rows, :128], back[rows, 128:]
                total_cos = total_cos + (back_cos * c - back_sin * s)
                total_sin = total_sin + (back_cos * s + back_sin * c)
            cos_one, sin_one = cosine[r, 16:, lanes], sine[r, 16:, lanes]
            part = factor[1 + r : 2 + r, lanes]
            lines[q * 4 + r] = jnp.sum(total_cos * cos_one - total_sin * sin_one, 0, keepdims=True) * part
            lines[q * 4 + 2 + r] = jnp.sum(total_cos * sin_one + total_sin * cos_one, 0, keepdims=True) * -part
    back = swap_fours(jnp.concatenate(lines, 0))
    return grids[0], grids[1], back.astype(BF16).astype(F32)


def tables_kernel(place_ref, waves_ref, wave_ref, factor_ref, outer_ref, cos_ref, sin_ref):
    waves = waves_ref[...]
    here = (iota((4, 192), 0) == place_ref[0]) & (iota((4, 192), 1) == place_ref[1])
    own = jnp.where(here, waves.astype(F32), 0.0)
    own = jnp.sum(jnp.sum(own, 0, keepdims=True), 1, keepdims=True)
    wave_ref[...] = jnp.broadcast_to(own, (1, 128))
    order = slot_order(waves)
    lengths = [place_ref[2 + r].astype(F32) for r in range(2)]
    factor_ref[...] = factors(order, lengths)
    for r in range(2):
        outer_ref[r], cos_ref[r], sin_ref[r] = tables(order, lengths[r])


def legendre_in_kernel(wave_ref, spec_ref, leg_ref, out_ref):
    wave = wave_ref[:, :1].astype(jnp.int32)
    out_ref[...] = legendre_in(spec_ref[0, 0], leg_ref[0, 0], wave).reshape(YX, 1, 128)


def turn_in_kernel(got_ref, out_ref):
    out_ref[...] = turn(got_ref[...].reshape(YX, 128))[:ZC].reshape(ZC, 1, 128)


def grid_kernel(got_ref, factor_ref, outer_ref, cos_ref, sin_ref, rows_ref, out_ref):
    one, two, out = grid_rows(
        got_ref[...].reshape(ZC, 128), factor_ref, outer_ref, cos_ref, sin_ref
    )
    rows_ref[0] = one
    rows_ref[1] = two
    out_ref[...] = out.reshape(ZC, 1, 128)


def turn_out_kernel(got_ref, out_ref):
    got = jnp.concatenate([got_ref[...].reshape(ZC, 128), jnp.zeros((YX - ZC, 128), F32)], 0)
    out_ref[...] = turn(got).reshape(YX, 1, 128)


def legendre_out_kernel(wave_ref, weight_ref, got_ref, leg_ref, rows_ref, out_ref, grid_ref):
    for a in range(NA):
        grid_ref[0, :, a * NB : (a + 1) * NB] = rows_ref[:, a, :].astype(BF16)
    wave = wave_ref[:, :1].astype(jnp.int32)
    weight = weight_ref[...].reshape(1, NLAT)
    real, imag = legendre_out(got_ref[...].reshape(YX, 128), weight, leg_ref[0, 0], wave)
    out_ref[0, 0, :, :NDEG] = real.astype(BF16)
    out_ref[0, 0, :, NDEG:] = imag.astype(BF16)


VMEM = pl.BlockSpec(memory_space=pltpu.VMEM)
SMEM = pl.BlockSpec(memory_space=pltpu.SMEM)


def call(kernel, name, in_specs, outs, flops=10**6):
    single = not isinstance(outs, list)
    return pl.pallas_call(
        kernel,
        name=name,
        in_specs=in_specs,
        out_specs=VMEM if single else [VMEM] * len(outs),
        out_shape=outs if single else tuple(outs),
        compiler_params=pltpu.CompilerParams(vmem_limit_bytes=24 * 1024 * 1024),
        cost_estimate=pl.CostEstimate(flops=flops, bytes_accessed=100000, transcendentals=0),
    )


def shape(*dims, dtype=F32):
    return jax.ShapeDtypeStruct(dims, dtype)


def shards(spectral_in, legendre, slot_wave, row_length, quad_weight):
    lat_index = (lax.axis_index("z") * 8 + lax.axis_index("y")) * 2 + lax.axis_index("c")
    place = jnp.concatenate([jnp.stack([lax.axis_index("x"), lat_index]).astype(jnp.int32), row_length])
    wave, factor, outer, cosine, sine = call(
        tables_kernel,
        "tables",
        [SMEM, VMEM],
        [
            shape(1, 128),
            shape(8, SLOTS),
            shape(2, 2 * NA_PAD, 2 * SLOTS, dtype=BF16),
            shape(2, 24, SLOTS),
            shape(2, 24, SLOTS),
        ],
        2 * 10**9,
    )(place, slot_wave)
    to_send = call(legendre_in_kernel, "legendre_in", [VMEM] * 3, shape(YX, 1, 128))(
        wave, spectral_in, legendre
    )
    got = lax.all_to_all(to_send, ("x", "y"), 0, 0, tiled=True)
    to_send = call(turn_in_kernel, "turn_in", [VMEM], shape(ZC, 1, 128))(got)
    got = lax.all_to_all(to_send, ("z", "c"), 0, 0, tiled=True)
    rows, to_send = call(
        grid_kernel, "grid", [VMEM] * 5, [shape(2, NA_PAD, NB), shape(ZC, 1, 128)]
    )(got, factor, outer, cosine, sine)
    got = lax.all_to_all(to_send, ("z", "c"), 0, 0, tiled=True)
    to_send = call(turn_out_kernel, "turn_out", [VMEM], shape(YX, 1, 128))(got)
    got = lax.all_to_all(to_send, ("x", "y"), 0, 0, tiled=True)
    spectral_out, grid_field = call(
        legendre_out_kernel,
        "legendre_out",
        [VMEM] * 5,
        [shape(1, 1, 4, 2 * NDEG, dtype=BF16), shape(1, 2, NLON, dtype=BF16)],
    )(wave, quad_weight, got, legendre, rows)
    return grid_field, spectral_out


def solution(mesh):
    cut = Mesh(mesh.devices.reshape(12, 8, 2, 4), ("z", "y", "c", "x"))
    lat = ("z", "y", "c")
    in_specs = (P("x", lat, None, None), P("x", lat, None, None), P(), P(lat), P())
    out_specs = (P("x", lat, None), P("x", lat, None, None))
    return jax.shard_map(shards, mesh=cut, in_specs=in_specs, out_specs=out_specs, check_vma=False)
```

```python
import math

import jax
import jax.numpy as jnp
from jax import lax
from jax.experimental import pallas as pl
from jax.experimental.pallas import tpu as pltpu
from jax.sharding import Mesh
from jax.sharding import PartitionSpec as P

M = 640
NDEG = 640
NLAT = 384
NLON = 2688
SLOTS = 768
ZC = 24
YX = 32
NB = 128
NA = 21
NA_PAD = 24
NT = 48

PARTS = [slice(q * 128, (q + 1) * 128) for q in range(6)]

F32 = jnp.float32
BF16 = jnp.bfloat16


def iota(shape, dim):
    return lax.broadcasted_iota(jnp.int32, shape, dim)


def dot(x, y, dims=((1,), (0,))):
    return lax.dot_general(x, y, (dims, ((), ())), preferred_element_type=F32)


def one_hot(cond):
    return jnp.where(cond, 1.0, 0.0).astype(BF16)


def row_selector():
    l = iota((NLAT, 128), 0)
    lane = iota((NLAT, 128), 1)
    return one_hot((lane & 63) == ((l & 1) * 32 + (l >> 5) * 2 + ((l >> 1) & 1)))


def legendre_in(spec, leg, wave, select):
    both = jnp.concatenate([spec[:, :NDEG].astype(F32), spec[:, NDEG:].astype(F32)], 0)
    kept = jnp.where(iota(both.shape, 1) >= wave, both, 0.0).astype(BF16)
    four = dot(kept, leg).astype(BF16).astype(F32)
    mine = ((iota((8, NLAT), 1) >> 2) & 7) == iota((8, NLAT), 0)
    spread = jnp.concatenate([jnp.where(mine, four[q : q + 1], 0.0) for q in range(8)], 0)
    moved = dot(spread.astype(BF16), select)
    return jnp.where(iota((YX, 128), 1) < 64, moved[:YX], moved[YX:])


def legendre_out(got, weight, leg, wave, select):
    low = iota((YX, 128), 1) < 64
    spread = jnp.concatenate([jnp.where(low, got, 0.0), jnp.where(low, 0.0, got)], 0)
    moved = dot(spread.astype(BF16), select, ((1,), (1,)))
    mine = ((iota((8, NLAT), 1) >> 2) & 7) == iota((8, NLAT), 0)
    rows = [
        jnp.sum(jnp.where(mine, moved[q * 8 : (q + 1) * 8], 0.0), 0, keepdims=True) for q in range(8)
    ]
    weighted = (jnp.concatenate(rows, 0) * weight).astype(BF16)
    result = dot(weighted, leg, ((1,), (1,)))
    result = jnp.where(iota(result.shape, 1) >= wave, result, 0.0)
    return result[:4], result[4:]


def turn(got):
    flipped = jnp.concatenate([got] * 4, 0).T
    group = iota((32, 128), 1) >> 5
    out = flipped[:32]
    for q in range(1, 4):
        out = jnp.where(group == q, flipped[q * 32 : (q + 1) * 32], out)
    return out


def roll(x, shift, axis):
    return pltpu.roll(x, shift % x.shape[axis], axis)


def swap_fours(x):
    line = iota(x.shape, 0) & 3
    group = iota(x.shape, 1) >> 5
    out = x
    for d in range(1, 4):
        moved = roll(x, -32 * d, 1)
        out = jnp.where(line - group == d, roll(moved, d, 0), out)
        out = jnp.where(line - group == d - 4, roll(moved, d - 4, 0), out)
    return out


def slot_selector():
    k = iota((192, 128), 0) & 31
    lane = iota((192, 128), 1)
    return one_hot(k == ((lane >> 6) * 16 + (lane & 7) * 2 + ((lane >> 5) & 1)))


def slot_order(waves, pick):
    both = jnp.concatenate([(waves >> 3).astype(F32), (waves & 7).astype(F32)], 0)
    part = iota((8, 192), 1) >> 5
    spread = jnp.concatenate([jnp.where(part == q, both, 0.0) for q in range(6)], 0)
    moved = dot(spread.astype(BF16), pick)
    row = iota((8, 128), 0)
    scale = jnp.where((row & 3) == ((iota((8, 128), 1) >> 3) & 3), jnp.where(row < 4, 8.0, 1.0), 0.0)
    return jnp.concatenate(
        [jnp.sum(moved[q * 8 : (q + 1) * 8] * scale, 0, keepdims=True) for q in range(6)], 1
    )


SIN_TERMS = [(-1.0) ** n * math.pi ** (2 * n + 1) / math.factorial(2 * n + 1) for n in range(7)]
COS_TERMS = [(-1.0) ** n * math.pi ** (2 * n) / math.factorial(2 * n) for n in range(8)]


def circle(points, waves, length):
    product = points * waves
    inverse = 1.0 / length
    rest = product - jnp.floor(product * inverse + 0.5) * length
    turn = rest * inverse
    square = turn * turn
    sine = jnp.full_like(square, SIN_TERMS[-1])
    for term in SIN_TERMS[-2::-1]:
        sine = sine * square + term
    sine = sine * turn
    cosine = jnp.full_like(square, COS_TERMS[-1])
    for term in COS_TERMS[-2::-1]:
        cosine = cosine * square + term
    return 1.0 - 2.0 * sine * sine, 2.0 * sine * cosine


def split(x):
    high = x.astype(BF16)
    return high, (x - high.astype(F32)).astype(BF16)


def tables(waves, length):
    row = iota((48, SLOTS), 0)
    points = jnp.where(row < NA_PAD, row * NB, jnp.where(row < 40, (row - NA_PAD) * 8, row - 40))
    cosine, sine = circle(points.astype(F32), waves, length)
    parts = []
    for lanes in PARTS:
        parts += [cosine[:NA_PAD, lanes], sine[:NA_PAD, lanes]]
    high, low = split(jnp.concatenate(parts, 1))
    outer = jnp.concatenate([high.astype(F32), low.astype(F32)], 0).astype(BF16)
    return outer, cosine[NA_PAD:], sine[NA_PAD:]


def factors(waves, lengths):
    empty = waves >= float(M)
    rows = [jnp.where(empty, 0.0, jnp.where(waves == 0.0, 1.0, 2.0))]
    rows += [jnp.where(empty, 0.0, 1.0 / n) for n in lengths]
    rows += [jnp.broadcast_to(n, waves.shape) for n in lengths]
    return jnp.concatenate(rows + [jnp.zeros((3, SLOTS), F32)], 0)


def grid_rows(got, factor, outer, cosine, sine):
    got = swap_fours(got)
    raws = [jnp.zeros((NB, NT), F32) for _ in range(2)]
    for q, lanes in enumerate(PARTS):
        for r in range(2):
            wide = slice(q * 256, (q + 1) * 256)
            cos_one, sin_one = cosine[r, 16:, lanes], sine[r, 16:, lanes]
            real = got[q * 4 + r : q * 4 + r + 1] * factor[0:1, lanes]
            imag = got[q * 4 + 2 + r : q * 4 + 3 + r] * factor[0:1, lanes]
            start_real = real * cos_one - imag * sin_one
            start_imag = real * sin_one + imag * cos_one
            mixed = []
            for j in range(16):
                c, s = cosine[r, j : j + 1, lanes], sine[r, j : j + 1, lanes]
                mixed.append(
                    jnp.concatenate([start_real * c - start_imag * s, -(start_real * s + start_imag * c)], 1)
                )
            high = jnp.concatenate(mixed, 0).astype(BF16)
            raws[r] = raws[r] + dot(high, outer[r, :, wide], ((1,), (1,)))
    grids, flips = [], []
    for r in range(2):
        raw = raws[r].T
        raw = raw[:NA_PAD] + raw[NA_PAD:]
        shaped = raw * (1.0 + 0.5 * jnp.tanh(raw))
        point = iota((NA_PAD, NB), 0) * NB + iota((NA_PAD, NB), 1)
        shaped = jnp.where(point.astype(F32) < factor[3 + r : 4 + r, :NB], shaped, 0.0)
        rounded = shaped.astype(BF16).astype(F32)
        grids.append(rounded)
        flips.append(jnp.concatenate([rounded, rounded], 0).T.astype(BF16))
    lines = [None] * 24
    for q, lanes in enumerate(PARTS):
        for r in range(2):
            wide = slice(q * 256, (q + 1) * 256)
            back = dot(flips[r], outer[r, :, wide])
            total_cos = jnp.zeros((8, 128), F32)
            total_sin = jnp.zeros((8, 128), F32)
            for j in range(16):
                c, s = cosine[r, j : j + 1, lanes], sine[r, j : j + 1, lanes]
                rows = slice(j * 8, (j + 1) * 8)
                back_cos, back_sin = back[rows, :128], back[rows, 128:]
                total_cos = total_cos + (back_cos * c - back_sin * s)
                total_sin = total_sin + (back_cos * s + back_sin * c)
            cos_one, sin_one = cosine[r, 16:, lanes], sine[r, 16:, lanes]
            part = factor[1 + r : 2 + r, lanes]
            lines[q * 4 + r] = jnp.sum(total_cos * cos_one - total_sin * sin_one, 0, keepdims=True) * part
            lines[q * 4 + 2 + r] = jnp.sum(total_cos * sin_one + total_sin * cos_one, 0, keepdims=True) * -part
    back = swap_fours(jnp.concatenate(lines, 0))
    return grids[0], grids[1], back.astype(BF16).astype(F32)


def select_kernel(pick_ref, select_ref):
    pick_ref[...] = slot_selector()
    select_ref[...] = row_selector()


def tables_kernel(place_ref, waves_ref, length_ref, pick_ref, wave_ref, factor_ref, outer_ref, cos_ref, sin_ref):
    waves = waves_ref[...]
    place = place_ref[...].reshape(1, 2)
    length = length_ref[...].reshape(1, 2)
    here = (iota((4, 192), 0) == place[:, :1]) & (iota((4, 192), 1) == place[:, 1:2])
    own = jnp.where(here, waves.astype(F32), 0.0)
    own = jnp.sum(jnp.sum(own, 0, keepdims=True), 1, keepdims=True)
    wave_ref[...] = jnp.broadcast_to(own, (1, 128))
    order = slot_order(waves, pick_ref[...])
    lengths = [length[:, r : r + 1].astype(F32) for r in range(2)]
    factor_ref[...] = factors(order, lengths)
    for r in range(2):
        outer_ref[r], cos_ref[r], sin_ref[r] = tables(order, lengths[r])


def legendre_in_kernel(wave_ref, select_ref, spec_ref, leg_ref, out_ref):
    wave = wave_ref[:, :1].astype(jnp.int32)
    out_ref[...] = legendre_in(spec_ref[0, 0], leg_ref[0, 0], wave, select_ref[...]).reshape(YX, 1, 128)


def turn_in_kernel(got_ref, out_ref):
    out_ref[...] = turn(got_ref[...].reshape(YX, 128))[:ZC].reshape(ZC, 1, 128)


def grid_kernel(got_ref, factor_ref, outer_ref, cos_ref, sin_ref, rows_ref, out_ref):
    one, two, out = grid_rows(
        got_ref[...].reshape(ZC, 128), factor_ref, outer_ref, cos_ref, sin_ref
    )
    rows_ref[0] = one
    rows_ref[1] = two
    out_ref[...] = out.reshape(ZC, 1, 128)


def turn_out_kernel(got_ref, out_ref):
    got = jnp.concatenate([got_ref[...].reshape(ZC, 128), jnp.zeros((YX - ZC, 128), F32)], 0)
    out_ref[...] = turn(got).reshape(YX, 1, 128)


def legendre_out_kernel(wave_ref, select_ref, weight_ref, got_ref, leg_ref, rows_ref, out_ref, grid_ref):
    for a in range(NA):
        grid_ref[0, :, a * NB : (a + 1) * NB] = rows_ref[:, a, :].astype(BF16)
    wave = wave_ref[:, :1].astype(jnp.int32)
    weight = weight_ref[...].reshape(1, NLAT)
    real, imag = legendre_out(got_ref[...].reshape(YX, 128), weight, leg_ref[0, 0], wave, select_ref[...])
    out_ref[0, 0, :, :NDEG] = real.astype(BF16)
    out_ref[0, 0, :, NDEG:] = imag.astype(BF16)


VMEM = pl.BlockSpec(memory_space=pltpu.VMEM)
SMEM = pl.BlockSpec(memory_space=pltpu.SMEM)


def call(kernel, name, in_specs, outs, flops=10**6):
    single = not isinstance(outs, list)
    return pl.pallas_call(
        kernel,
        name=name,
        in_specs=in_specs,
        out_specs=VMEM if single else [VMEM] * len(outs),
        out_shape=outs if single else tuple(outs),
        compiler_params=pltpu.CompilerParams(vmem_limit_bytes=24 * 1024 * 1024),
        cost_estimate=pl.CostEstimate(flops=flops, bytes_accessed=100000, transcendentals=0),
    )


def shape(*dims, dtype=F32):
    return jax.ShapeDtypeStruct(dims, dtype)


def shards(spectral_in, legendre, slot_wave, row_length, quad_weight):
    lat_index = (lax.axis_index("z") * 8 + lax.axis_index("y")) * 2 + lax.axis_index("c")
    place = jnp.stack([lax.axis_index("x"), lat_index]).astype(jnp.int32)
    pick, select = call(
        select_kernel, "select", [], [shape(192, 128, dtype=BF16), shape(NLAT, 128, dtype=BF16)], 2 * 10**9
    )()
    wave, factor, outer, cosine, sine = call(
        tables_kernel,
        "tables",
        [VMEM] * 4,
        [
            shape(1, 128),
            shape(8, SLOTS),
            shape(2, 2 * NA_PAD, 2 * SLOTS, dtype=BF16),
            shape(2, 24, SLOTS),
            shape(2, 24, SLOTS),
        ],
        10**6,
    )(place, slot_wave, row_length, pick)
    to_send = call(legendre_in_kernel, "legendre_in", [VMEM] * 4, shape(YX, 1, 128))(
        wave, select, spectral_in, legendre
    )
    got = lax.all_to_all(to_send, ("x", "y"), 0, 0, tiled=True)
    to_send = call(turn_in_kernel, "turn_in", [VMEM], shape(ZC, 1, 128))(got)
    got = lax.all_to_all(to_send, ("z", "c"), 0, 0, tiled=True)
    rows, to_send = call(
        grid_kernel, "grid", [VMEM] * 5, [shape(2, NA_PAD, NB), shape(ZC, 1, 128)]
    )(got, factor, outer, cosine, sine)
    got = lax.all_to_all(to_send, ("z", "c"), 0, 0, tiled=True)
    to_send = call(turn_out_kernel, "turn_out", [VMEM], shape(YX, 1, 128))(got)
    got = lax.all_to_all(to_send, ("x", "y"), 0, 0, tiled=True)
    spectral_out, grid_field = call(
        legendre_out_kernel,
        "legendre_out",
        [VMEM] * 6,
        [shape(1, 1, 4, 2 * NDEG, dtype=BF16), shape(1, 2, NLON, dtype=BF16)],
    )(wave, select, quad_weight, got, legendre, rows)
    return grid_field, spectral_out


def solution(mesh):
    cut = Mesh(mesh.devices.reshape(12, 8, 2, 4), ("z", "y", "c", "x"))
    lat = ("z", "y", "c")
    in_specs = (P("x", lat, None, None), P("x", lat, None, None), P(), P(lat), P())
    out_specs = (P("x", lat, None), P("x", lat, None, None))
    return jax.shard_map(shards, mesh=cut, in_specs=in_specs, out_specs=out_specs, check_vma=False)
```

```python
import math

import jax
import jax.numpy as jnp
from jax import lax
from jax.experimental import pallas as pl
from jax.experimental.pallas import tpu as pltpu
from jax.sharding import Mesh
from jax.sharding import PartitionSpec as P

M = 640
NDEG = 640
NLAT = 384
NLON = 2688
SLOTS = 768
ZC = 24
YX = 32
NB = 128
NA = 21
NA_PAD = 24
NT = 48

PARTS = [slice(q * 128, (q + 1) * 128) for q in range(6)]

F32 = jnp.float32
BF16 = jnp.bfloat16


def iota(shape, dim):
    return lax.broadcasted_iota(jnp.int32, shape, dim)


def dot(x, y, dims=((1,), (0,))):
    return lax.dot_general(x, y, (dims, ((), ())), preferred_element_type=F32)


def one_hot(cond):
    return jnp.where(cond, 1.0, 0.0).astype(BF16)


def row_selector():
    l = iota((NLAT, 128), 0)
    lane = iota((NLAT, 128), 1)
    return one_hot((lane & 63) == ((l & 1) * 32 + (l >> 5) * 2 + ((l >> 1) & 1)))


def legendre_in(spec, leg, wave, select):
    both = jnp.concatenate([spec[:, :NDEG].astype(F32), spec[:, NDEG:].astype(F32)], 0)
    kept = jnp.where(iota(both.shape, 1) >= wave, both, 0.0).astype(BF16)
    four = dot(kept, leg).astype(BF16).astype(F32)
    mine = ((iota((8, NLAT), 1) >> 2) & 7) == iota((8, NLAT), 0)
    spread = jnp.concatenate([jnp.where(mine, four[q : q + 1], 0.0) for q in range(8)], 0)
    moved = dot(spread.astype(BF16), select)
    return jnp.where(iota((YX, 128), 1) < 64, moved[:YX], moved[YX:])


def legendre_out(got, weight, leg, wave, select):
    low = iota((YX, 128), 1) < 64
    spread = jnp.concatenate([jnp.where(low, got, 0.0), jnp.where(low, 0.0, got)], 0)
    moved = dot(spread.astype(BF16), select, ((1,), (1,)))
    mine = ((iota((8, NLAT), 1) >> 2) & 7) == iota((8, NLAT), 0)
    rows = [
        jnp.sum(jnp.where(mine, moved[q * 8 : (q + 1) * 8], 0.0), 0, keepdims=True) for q in range(8)
    ]
    weighted = (jnp.concatenate(rows, 0) * weight).astype(BF16)
    result = dot(weighted, leg, ((1,), (1,)))
    result = jnp.where(iota(result.shape, 1) >= wave, result, 0.0)
    return result[:4], result[4:]


def turn(got):
    flipped = jnp.concatenate([got] * 4, 0).T
    group = iota((32, 128), 1) >> 5
    out = flipped[:32]
    for q in range(1, 4):
        out = jnp.where(group == q, flipped[q * 32 : (q + 1) * 32], out)
    return out


def roll(x, shift, axis):
    return pltpu.roll(x, shift % x.shape[axis], axis)


def swap_fours(x):
    line = iota(x.shape, 0) & 3
    group = iota(x.shape, 1) >> 5
    out = x
    for d in range(1, 4):
        moved = roll(x, -32 * d, 1)
        out = jnp.where(line - group == d, roll(moved, d, 0), out)
        out = jnp.where(line - group == d - 4, roll(moved, d - 4, 0), out)
    return out


def slot_selector():
    k = iota((192, 128), 0) & 31
    lane = iota((192, 128), 1)
    return one_hot(k == ((lane >> 6) * 16 + (lane & 7) * 2 + ((lane >> 5) & 1)))


def slot_order(waves, pick):
    both = jnp.concatenate([(waves >> 3).astype(F32), (waves & 7).astype(F32)], 0)
    part = iota((8, 192), 1) >> 5
    spread = jnp.concatenate([jnp.where(part == q, both, 0.0) for q in range(6)], 0)
    moved = dot(spread.astype(BF16), pick)
    row = iota((8, 128), 0)
    scale = jnp.where((row & 3) == ((iota((8, 128), 1) >> 3) & 3), jnp.where(row < 4, 8.0, 1.0), 0.0)
    return jnp.concatenate(
        [jnp.sum(moved[q * 8 : (q + 1) * 8] * scale, 0, keepdims=True) for q in range(6)], 1
    )


SIN_TERMS = [(-1.0) ** n * math.pi ** (2 * n + 1) / math.factorial(2 * n + 1) for n in range(7)]
COS_TERMS = [(-1.0) ** n * math.pi ** (2 * n) / math.factorial(2 * n) for n in range(8)]


def circle(points, waves, length):
    product = points * waves
    inverse = 1.0 / length
    rest = product - jnp.floor(product * inverse + 0.5) * length
    turn = rest * inverse
    square = turn * turn
    sine = jnp.full_like(square, SIN_TERMS[-1])
    for term in SIN_TERMS[-2::-1]:
        sine = sine * square + term
    sine = sine * turn
    cosine = jnp.full_like(square, COS_TERMS[-1])
    for term in COS_TERMS[-2::-1]:
        cosine = cosine * square + term
    return 1.0 - 2.0 * sine * sine, 2.0 * sine * cosine


def split(x):
    high = x.astype(BF16)
    return high, (x - high.astype(F32)).astype(BF16)


def tables(waves, length):
    row = iota((48, SLOTS), 0)
    points = jnp.where(row < NA_PAD, row * NB, jnp.where(row < 40, (row - NA_PAD) * 8, row - 40))
    cosine, sine = circle(points.astype(F32), waves, length)
    parts = []
    for lanes in PARTS:
        parts += [cosine[:NA_PAD, lanes], sine[:NA_PAD, lanes]]
    high, low = split(jnp.concatenate(parts, 1))
    outer = jnp.concatenate([high.astype(F32), low.astype(F32)], 0).astype(BF16)
    return outer, cosine[NA_PAD:], sine[NA_PAD:]


def factors(waves, lengths):
    empty = waves >= float(M)
    rows = [jnp.where(empty, 0.0, jnp.where(waves == 0.0, 1.0, 2.0))]
    rows += [jnp.where(empty, 0.0, 1.0 / n) for n in lengths]
    rows += [jnp.broadcast_to(n, waves.shape) for n in lengths]
    return jnp.concatenate(rows + [jnp.zeros((3, SLOTS), F32)], 0)


def grid_rows(got, factor, outer, cosine, sine):
    got = swap_fours(got)
    raws = [jnp.zeros((NB, NT), F32) for _ in range(2)]
    for q, lanes in enumerate(PARTS):
        for r in range(2):
            wide = slice(q * 256, (q + 1) * 256)
            cos_one, sin_one = cosine[r, 16:, lanes], sine[r, 16:, lanes]
            real = got[q * 4 + r : q * 4 + r + 1] * factor[0:1, lanes]
            imag = got[q * 4 + 2 + r : q * 4 + 3 + r] * factor[0:1, lanes]
            start_real = real * cos_one - imag * sin_one
            start_imag = real * sin_one + imag * cos_one
            mixed = []
            for j in range(16):
                c, s = cosine[r, j : j + 1, lanes], sine[r, j : j + 1, lanes]
                mixed.append(
                    jnp.concatenate([start_real * c - start_imag * s, -(start_real * s + start_imag * c)], 1)
                )
            high = jnp.concatenate(mixed, 0).astype(BF16)
            raws[r] = raws[r] + dot(high, outer[r, :, wide], ((1,), (1,)))
    grids, flips = [], []
    for r in range(2):
        raw = raws[r].T
        raw = raw[:NA_PAD] + raw[NA_PAD:]
        shaped = raw * (1.0 + 0.5 * jnp.tanh(raw))
        point = iota((NA_PAD, NB), 0) * NB + iota((NA_PAD, NB), 1)
        shaped = jnp.where(point.astype(F32) < factor[3 + r : 4 + r, :NB], shaped, 0.0)
        rounded = shaped.astype(BF16).astype(F32)
        grids.append(rounded)
        flips.append(jnp.concatenate([rounded, rounded], 0).T.astype(BF16))
    lines = [None] * 24
    for q, lanes in enumerate(PARTS):
        for r in range(2):
            wide = slice(q * 256, (q + 1) * 256)
            back = dot(flips[r], outer[r, :, wide])
            total_cos = jnp.zeros((8, 128), F32)
            total_sin = jnp.zeros((8, 128), F32)
            for j in range(16):
                c, s = cosine[r, j : j + 1, lanes], sine[r, j : j + 1, lanes]
                rows = slice(j * 8, (j + 1) * 8)
                back_cos, back_sin = back[rows, :128], back[rows, 128:]
                total_cos = total_cos + (back_cos * c - back_sin * s)
                total_sin = total_sin + (back_cos * s + back_sin * c)
            cos_one, sin_one = cosine[r, 16:, lanes], sine[r, 16:, lanes]
            part = factor[1 + r : 2 + r, lanes]
            lines[q * 4 + r] = jnp.sum(total_cos * cos_one - total_sin * sin_one, 0, keepdims=True) * part
            lines[q * 4 + 2 + r] = jnp.sum(total_cos * sin_one + total_sin * cos_one, 0, keepdims=True) * -part
    back = swap_fours(jnp.concatenate(lines, 0))
    return grids[0], grids[1], back.astype(BF16).astype(F32)


def select_kernel(pick_ref, select_ref):
    pick_ref[...] = slot_selector()
    select_ref[...] = row_selector()


def start_kernel(
    waves_ref, length_ref, weight_ref, pick_ref, select_ref, spec_ref, leg_ref,
    out_ref, wave_ref, line_ref, factor_ref, outer_ref, cos_ref, sin_ref,
):
    waves = waves_ref[...]
    length = length_ref[...].reshape(1, 2)
    lat_index = (lax.axis_index("z") * 8 + lax.axis_index("y")) * 2 + lax.axis_index("c")
    here = (iota((4, 192), 0) == lax.axis_index("x")) & (iota((4, 192), 1) == lat_index)
    own = jnp.where(here, waves.astype(F32), 0.0)
    own = jnp.sum(jnp.sum(own, 0, keepdims=True), 1, keepdims=True)
    wave_ref[...] = jnp.broadcast_to(own, (1, 128))
    line_ref[...] = weight_ref[...].reshape(1, NLAT)
    order = slot_order(waves, pick_ref[...])
    lengths = [length[:, r : r + 1].astype(F32) for r in range(2)]
    factor_ref[...] = factors(order, lengths)
    for r in range(2):
        outer_ref[r], cos_ref[r], sin_ref[r] = tables(order, lengths[r])
    out = legendre_in(spec_ref[0, 0], leg_ref[0, 0], own.astype(jnp.int32), select_ref[...])
    out_ref[...] = out.reshape(YX, 1, 128)


def turn_in_kernel(got_ref, out_ref):
    out_ref[...] = turn(got_ref[...].reshape(YX, 128))[:ZC].reshape(ZC, 1, 128)


def grid_kernel(got_ref, factor_ref, outer_ref, cos_ref, sin_ref, rows_ref, out_ref):
    one, two, out = grid_rows(
        got_ref[...].reshape(ZC, 128), factor_ref, outer_ref, cos_ref, sin_ref
    )
    rows_ref[0] = one
    rows_ref[1] = two
    out_ref[...] = out.reshape(ZC, 1, 128)


def turn_out_kernel(got_ref, out_ref):
    got = jnp.concatenate([got_ref[...].reshape(ZC, 128), jnp.zeros((YX - ZC, 128), F32)], 0)
    out_ref[...] = turn(got).reshape(YX, 1, 128)


def legendre_out_kernel(wave_ref, select_ref, weight_ref, got_ref, leg_ref, rows_ref, out_ref, grid_ref):
    for a in range(NA):
        grid_ref[0, :, a * NB : (a + 1) * NB] = rows_ref[:, a, :].astype(BF16)
    wave = wave_ref[:, :1].astype(jnp.int32)
    real, imag = legendre_out(got_ref[...].reshape(YX, 128), weight_ref[...], leg_ref[0, 0], wave, select_ref[...])
    out_ref[0, 0, :, :NDEG] = real.astype(BF16)
    out_ref[0, 0, :, NDEG:] = imag.astype(BF16)


VMEM = pl.BlockSpec(memory_space=pltpu.VMEM)
SMEM = pl.BlockSpec(memory_space=pltpu.SMEM)


def call(kernel, name, in_specs, outs, flops=10**6):
    single = not isinstance(outs, list)
    return pl.pallas_call(
        kernel,
        name=name,
        in_specs=in_specs,
        out_specs=VMEM if single else [VMEM] * len(outs),
        out_shape=outs if single else tuple(outs),
        compiler_params=pltpu.CompilerParams(vmem_limit_bytes=24 * 1024 * 1024),
        cost_estimate=pl.CostEstimate(flops=flops, bytes_accessed=100000, transcendentals=0),
    )


def shape(*dims, dtype=F32):
    return jax.ShapeDtypeStruct(dims, dtype)


def shards(spectral_in, legendre, slot_wave, row_length, quad_weight):
    pick, select = call(
        select_kernel, "select", [], [shape(192, 128, dtype=BF16), shape(NLAT, 128, dtype=BF16)], 2 * 10**9
    )()
    to_send, wave, weight, factor, outer, cosine, sine = call(
        start_kernel,
        "start",
        [VMEM] * 7,
        [
            shape(YX, 1, 128),
            shape(1, 128),
            shape(1, NLAT),
            shape(8, SLOTS),
            shape(2, 2 * NA_PAD, 2 * SLOTS, dtype=BF16),
            shape(2, 24, SLOTS),
            shape(2, 24, SLOTS),
        ],
    )(slot_wave, row_length, quad_weight, pick, select, spectral_in, legendre)
    got = lax.all_to_all(to_send, ("x", "y"), 0, 0, tiled=True)
    to_send = call(turn_in_kernel, "turn_in", [VMEM], shape(ZC, 1, 128))(got)
    got = lax.all_to_all(to_send, ("z", "c"), 0, 0, tiled=True)
    rows, to_send = call(
        grid_kernel, "grid", [VMEM] * 5, [shape(2, NA_PAD, NB), shape(ZC, 1, 128)]
    )(got, factor, outer, cosine, sine)
    got = lax.all_to_all(to_send, ("z", "c"), 0, 0, tiled=True)
    to_send = call(turn_out_kernel, "turn_out", [VMEM], shape(YX, 1, 128))(got)
    got = lax.all_to_all(to_send, ("x", "y"), 0, 0, tiled=True)
    spectral_out, grid_field = call(
        legendre_out_kernel,
        "legendre_out",
        [VMEM] * 6,
        [shape(1, 1, 4, 2 * NDEG, dtype=BF16), shape(1, 2, NLON, dtype=BF16)],
    )(wave, select, weight, got, legendre, rows)
    return grid_field, spectral_out


def solution(mesh):
    cut = Mesh(mesh.devices.reshape(12, 8, 2, 4), ("z", "y", "c", "x"))
    lat = ("z", "y", "c")
    in_specs = (P("x", lat, None, None), P("x", lat, None, None), P(), P(lat), P())
    out_specs = (P("x", lat, None), P("x", lat, None, None))
    return jax.shard_map(shards, mesh=cut, in_specs=in_specs, out_specs=out_specs, check_vma=False)
```

```python
import math

import jax
import jax.numpy as jnp
from jax import lax
from jax.experimental import pallas as pl
from jax.experimental.pallas import tpu as pltpu
from jax.sharding import Mesh
from jax.sharding import PartitionSpec as P

M = 640
NDEG = 640
NLAT = 384
NLON = 2688
SLOTS = 768
ZC = 24
YX = 32
NB = 128
NA = 21
NA_PAD = 24
NT = 48

PARTS = [slice(q * 128, (q + 1) * 128) for q in range(6)]

F32 = jnp.float32
BF16 = jnp.bfloat16


def iota(shape, dim):
    return lax.broadcasted_iota(jnp.int32, shape, dim)


def dot(x, y, dims=((1,), (0,))):
    return lax.dot_general(x, y, (dims, ((), ())), preferred_element_type=F32)


def one_hot(cond):
    return jnp.where(cond, 1.0, 0.0).astype(BF16)


def row_selector():
    l = iota((NLAT, 128), 0)
    lane = iota((NLAT, 128), 1)
    return one_hot((lane & 63) == ((l & 1) * 32 + (l >> 5) * 2 + ((l >> 1) & 1)))


def legendre_in(spec, leg, wave, select):
    both = jnp.concatenate([spec[:, :NDEG].astype(F32), spec[:, NDEG:].astype(F32)], 0)
    kept = jnp.where(iota(both.shape, 1) >= wave, both, 0.0).astype(BF16)
    four = dot(kept, leg).astype(BF16).astype(F32)
    mine = ((iota((8, NLAT), 1) >> 2) & 7) == iota((8, NLAT), 0)
    spread = jnp.concatenate([jnp.where(mine, four[q : q + 1], 0.0) for q in range(8)], 0)
    moved = dot(spread.astype(BF16), select)
    return jnp.where(iota((YX, 128), 1) < 64, moved[:YX], moved[YX:])


def legendre_out(got, weight, leg, wave, select):
    low = iota((YX, 128), 1) < 64
    spread = jnp.concatenate([jnp.where(low, got, 0.0), jnp.where(low, 0.0, got)], 0)
    moved = dot(spread.astype(BF16), select, ((1,), (1,)))
    mine = ((iota((8, NLAT), 1) >> 2) & 7) == iota((8, NLAT), 0)
    rows = [
        jnp.sum(jnp.where(mine, moved[q * 8 : (q + 1) * 8], 0.0), 0, keepdims=True) for q in range(8)
    ]
    weighted = (jnp.concatenate(rows, 0) * weight).astype(BF16)
    result = dot(weighted, leg, ((1,), (1,)))
    result = jnp.where(iota(result.shape, 1) >= wave, result, 0.0)
    return result[:4], result[4:]


def turn(got):
    flipped = jnp.concatenate([got] * 4, 0).T
    group = iota((32, 128), 1) >> 5
    out = flipped[:32]
    for q in range(1, 4):
        out = jnp.where(group == q, flipped[q * 32 : (q + 1) * 32], out)
    return out


def roll(x, shift, axis):
    return pltpu.roll(x, shift % x.shape[axis], axis)


def swap_fours(x):
    line = iota(x.shape, 0) & 3
    group = iota(x.shape, 1) >> 5
    out = x
    for d in range(1, 4):
        moved = roll(x, -32 * d, 1)
        out = jnp.where(line - group == d, roll(moved, d, 0), out)
        out = jnp.where(line - group == d - 4, roll(moved, d - 4, 0), out)
    return out


def slot_selector():
    k = iota((192, 128), 0) & 31
    lane = iota((192, 128), 1)
    return one_hot(k == ((lane >> 6) * 16 + (lane & 7) * 2 + ((lane >> 5) & 1)))


def slot_order(waves, pick):
    both = jnp.concatenate([(waves >> 3).astype(F32), (waves & 7).astype(F32)], 0)
    part = iota((8, 192), 1) >> 5
    spread = jnp.concatenate([jnp.where(part == q, both, 0.0) for q in range(6)], 0)
    moved = dot(spread.astype(BF16), pick)
    row = iota((8, 128), 0)
    scale = jnp.where((row & 3) == ((iota((8, 128), 1) >> 3) & 3), jnp.where(row < 4, 8.0, 1.0), 0.0)
    return jnp.concatenate(
        [jnp.sum(moved[q * 8 : (q + 1) * 8] * scale, 0, keepdims=True) for q in range(6)], 1
    )


SIN_TERMS = [(-1.0) ** n * math.pi ** (2 * n + 1) / math.factorial(2 * n + 1) for n in range(7)]
COS_TERMS = [(-1.0) ** n * math.pi ** (2 * n) / math.factorial(2 * n) for n in range(8)]


def circle(points, waves, length):
    product = points * waves
    inverse = 1.0 / length
    rest = product - jnp.floor(product * inverse + 0.5) * length
    turn = rest * inverse
    square = turn * turn
    sine = jnp.full_like(square, SIN_TERMS[-1])
    for term in SIN_TERMS[-2::-1]:
        sine = sine * square + term
    sine = sine * turn
    cosine = jnp.full_like(square, COS_TERMS[-1])
    for term in COS_TERMS[-2::-1]:
        cosine = cosine * square + term
    return 1.0 - 2.0 * sine * sine, 2.0 * sine * cosine


def split(x):
    high = x.astype(BF16)
    return high, (x - high.astype(F32)).astype(BF16)


def tables(waves, length):
    row = iota((48, SLOTS), 0)
    points = jnp.where(row < NA_PAD, row * NB, jnp.where(row < 40, (row - NA_PAD) * 8, row - 40))
    cosine, sine = circle(points.astype(F32), waves, length)
    parts = []
    for lanes in PARTS:
        parts += [cosine[:NA_PAD, lanes], sine[:NA_PAD, lanes]]
    high, low = split(jnp.concatenate(parts, 1))
    outer = jnp.concatenate([high.astype(F32), low.astype(F32)], 0).astype(BF16)
    return outer, cosine[NA_PAD:], sine[NA_PAD:]


def factors(waves, lengths):
    empty = waves >= float(M)
    rows = [jnp.where(empty, 0.0, jnp.where(waves == 0.0, 1.0, 2.0))]
    rows += [jnp.where(empty, 0.0, 1.0 / n) for n in lengths]
    rows += [jnp.broadcast_to(n, waves.shape) for n in lengths]
    return jnp.concatenate(rows + [jnp.zeros((3, SLOTS), F32)], 0)


def grid_rows(got, factor, outer, cosine, sine):
    got = swap_fours(got)
    raws = [jnp.zeros((NB, NT), F32) for _ in range(2)]
    for q, lanes in enumerate(PARTS):
        for r in range(2):
            wide = slice(q * 256, (q + 1) * 256)
            cos_one, sin_one = cosine[r, 16:, lanes], sine[r, 16:, lanes]
            real = got[q * 4 + r : q * 4 + r + 1] * factor[0:1, lanes]
            imag = got[q * 4 + 2 + r : q * 4 + 3 + r] * factor[0:1, lanes]
            start_real = real * cos_one - imag * sin_one
            start_imag = real * sin_one + imag * cos_one
            mixed = []
            for j in range(16):
                c, s = cosine[r, j : j + 1, lanes], sine[r, j : j + 1, lanes]
                mixed.append(
                    jnp.concatenate([start_real * c - start_imag * s, -(start_real * s + start_imag * c)], 1)
                )
            high = jnp.concatenate(mixed, 0).astype(BF16)
            raws[r] = raws[r] + dot(high, outer[r, :, wide], ((1,), (1,)))
    grids, flips = [], []
    for r in range(2):
        raw = raws[r].T
        raw = raw[:NA_PAD] + raw[NA_PAD:]
        shaped = raw * (1.0 + 0.5 * jnp.tanh(raw))
        point = iota((NA_PAD, NB), 0) * NB + iota((NA_PAD, NB), 1)
        shaped = jnp.where(point.astype(F32) < factor[3 + r : 4 + r, :NB], shaped, 0.0)
        rounded = shaped.astype(BF16).astype(F32)
        grids.append(rounded)
        flips.append(jnp.concatenate([rounded, rounded], 0).T.astype(BF16))
    lines = [None] * 24
    for q, lanes in enumerate(PARTS):
        for r in range(2):
            wide = slice(q * 256, (q + 1) * 256)
            back = dot(flips[r], outer[r, :, wide])
            total_cos = jnp.zeros((8, 128), F32)
            total_sin = jnp.zeros((8, 128), F32)
            for j in range(16):
                c, s = cosine[r, j : j + 1, lanes], sine[r, j : j + 1, lanes]
                rows = slice(j * 8, (j + 1) * 8)
                back_cos, back_sin = back[rows, :128], back[rows, 128:]
                total_cos = total_cos + (back_cos * c - back_sin * s)
                total_sin = total_sin + (back_cos * s + back_sin * c)
            cos_one, sin_one = cosine[r, 16:, lanes], sine[r, 16:, lanes]
            part = factor[1 + r : 2 + r, lanes]
            lines[q * 4 + r] = jnp.sum(total_cos * cos_one - total_sin * sin_one, 0, keepdims=True) * part
            lines[q * 4 + 2 + r] = jnp.sum(total_cos * sin_one + total_sin * cos_one, 0, keepdims=True) * -part
    back = swap_fours(jnp.concatenate(lines, 0))
    return grids[0], grids[1], back.astype(BF16).astype(F32)


def select_kernel(pick_ref, select_ref):
    pick_ref[...] = slot_selector()
    select_ref[...] = row_selector()


def legendre_in_kernel(waves_ref, weight_ref, select_ref, spec_ref, leg_ref, out_ref, wave_ref, line_ref):
    lat_index = (lax.axis_index("z") * 8 + lax.axis_index("y")) * 2 + lax.axis_index("c")
    here = (iota((4, 192), 0) == lax.axis_index("x")) & (iota((4, 192), 1) == lat_index)
    own = jnp.where(here, waves_ref[...].astype(F32), 0.0)
    own = jnp.sum(jnp.sum(own, 0, keepdims=True), 1, keepdims=True)
    wave_ref[...] = jnp.broadcast_to(own, (1, 128))
    line_ref[...] = weight_ref[...].reshape(1, NLAT)
    out = legendre_in(spec_ref[0, 0], leg_ref[0, 0], own.astype(jnp.int32), select_ref[...])
    out_ref[...] = out.reshape(YX, 1, 128)


def tables_kernel(waves_ref, length_ref, pick_ref, factor_ref, outer_ref, cos_ref, sin_ref):
    length = length_ref[...].reshape(1, 2)
    order = slot_order(waves_ref[...], pick_ref[...])
    lengths = [length[:, r : r + 1].astype(F32) for r in range(2)]
    factor_ref[...] = factors(order, lengths)
    for r in range(2):
        outer_ref[r], cos_ref[r], sin_ref[r] = tables(order, lengths[r])


def turn_in_kernel(got_ref, out_ref):
    out_ref[...] = turn(got_ref[...].reshape(YX, 128))[:ZC].reshape(ZC, 1, 128)


def grid_kernel(got_ref, factor_ref, outer_ref, cos_ref, sin_ref, rows_ref, out_ref):
    one, two, out = grid_rows(
        got_ref[...].reshape(ZC, 128), factor_ref, outer_ref, cos_ref, sin_ref
    )
    rows_ref[0] = one
    rows_ref[1] = two
    out_ref[...] = out.reshape(ZC, 1, 128)


def turn_out_kernel(got_ref, out_ref):
    got = jnp.concatenate([got_ref[...].reshape(ZC, 128), jnp.zeros((YX - ZC, 128), F32)], 0)
    out_ref[...] = turn(got).reshape(YX, 1, 128)


def legendre_out_kernel(wave_ref, select_ref, weight_ref, got_ref, leg_ref, rows_ref, out_ref, grid_ref):
    for a in range(NA):
        grid_ref[0, :, a * NB : (a + 1) * NB] = rows_ref[:, a, :].astype(BF16)
    wave = wave_ref[:, :1].astype(jnp.int32)
    real, imag = legendre_out(got_ref[...].reshape(YX, 128), weight_ref[...], leg_ref[0, 0], wave, select_ref[...])
    out_ref[0, 0, :, :NDEG] = real.astype(BF16)
    out_ref[0, 0, :, NDEG:] = imag.astype(BF16)


VMEM = pl.BlockSpec(memory_space=pltpu.VMEM)
SMEM = pl.BlockSpec(memory_space=pltpu.SMEM)


def call(kernel, name, in_specs, outs, flops=10**6):
    single = not isinstance(outs, list)
    return pl.pallas_call(
        kernel,
        name=name,
        in_specs=in_specs,
        out_specs=VMEM if single else [VMEM] * len(outs),
        out_shape=outs if single else tuple(outs),
        compiler_params=pltpu.CompilerParams(vmem_limit_bytes=24 * 1024 * 1024),
        cost_estimate=pl.CostEstimate(flops=flops, bytes_accessed=100000, transcendentals=0),
    )


def shape(*dims, dtype=F32):
    return jax.ShapeDtypeStruct(dims, dtype)


def shards(spectral_in, legendre, slot_wave, row_length, quad_weight):
    pick, select = call(
        select_kernel, "select", [], [shape(192, 128, dtype=BF16), shape(NLAT, 128, dtype=BF16)], 2 * 10**9
    )()
    to_send, wave, weight = call(
        legendre_in_kernel, "legendre_in", [VMEM] * 5, [shape(YX, 1, 128), shape(1, 128), shape(1, NLAT)]
    )(slot_wave, quad_weight, select, spectral_in, legendre)
    factor, outer, cosine, sine = call(
        tables_kernel,
        "tables",
        [VMEM] * 3,
        [
            shape(8, SLOTS),
            shape(2, 2 * NA_PAD, 2 * SLOTS, dtype=BF16),
            shape(2, 24, SLOTS),
            shape(2, 24, SLOTS),
        ],
        2 * 10**9,
    )(slot_wave, row_length, pick)
    got = lax.all_to_all(to_send, ("x", "y"), 0, 0, tiled=True)
    to_send = call(turn_in_kernel, "turn_in", [VMEM], shape(ZC, 1, 128))(got)
    got = lax.all_to_all(to_send, ("z", "c"), 0, 0, tiled=True)
    rows, to_send = call(
        grid_kernel, "grid", [VMEM] * 5, [shape(2, NA_PAD, NB), shape(ZC, 1, 128)]
    )(got, factor, outer, cosine, sine)
    got = lax.all_to_all(to_send, ("z", "c"), 0, 0, tiled=True)
    to_send = call(turn_out_kernel, "turn_out", [VMEM], shape(YX, 1, 128))(got)
    got = lax.all_to_all(to_send, ("x", "y"), 0, 0, tiled=True)
    spectral_out, grid_field = call(
        legendre_out_kernel,
        "legendre_out",
        [VMEM] * 6,
        [shape(1, 1, 4, 2 * NDEG, dtype=BF16), shape(1, 2, NLON, dtype=BF16)],
    )(wave, select, weight, got, legendre, rows)
    return grid_field, spectral_out


def solution(mesh):
    cut = Mesh(mesh.devices.reshape(12, 8, 2, 4), ("z", "y", "c", "x"))
    lat = ("z", "y", "c")
    in_specs = (P("x", lat, None, None), P("x", lat, None, None), P(), P(lat), P())
    out_specs = (P("x", lat, None), P("x", lat, None, None))
    return jax.shard_map(shards, mesh=cut, in_specs=in_specs, out_specs=out_specs, check_vma=False)
```

```python
import math

import jax
import jax.numpy as jnp
from jax import lax
from jax.experimental import pallas as pl
from jax.experimental.pallas import tpu as pltpu
from jax.sharding import Mesh
from jax.sharding import PartitionSpec as P

M = 640
NDEG = 640
NLAT = 384
NLON = 2688
SLOTS = 768
ZC = 24
YX = 32
NB = 128
NA = 21
NA_PAD = 24
NT = 48

PARTS = [slice(q * 128, (q + 1) * 128) for q in range(6)]

F32 = jnp.float32
BF16 = jnp.bfloat16


def iota(shape, dim):
    return lax.broadcasted_iota(jnp.int32, shape, dim)


def dot(x, y, dims=((1,), (0,))):
    return lax.dot_general(x, y, (dims, ((), ())), preferred_element_type=F32)


def one_hot(cond):
    return jnp.where(cond, 1.0, 0.0).astype(BF16)


def row_selector():
    l = iota((NLAT, 128), 0)
    lane = iota((NLAT, 128), 1)
    return one_hot((lane & 63) == ((l & 1) * 32 + ((l >> 1) & 1) * 12 + (l >> 5)))


def legendre_in(spec, leg, wave, select):
    both = jnp.concatenate([spec[:, :NDEG].astype(F32), spec[:, NDEG:].astype(F32)], 0)
    kept = jnp.where(iota(both.shape, 1) >= wave, both, 0.0).astype(BF16)
    four = dot(kept, leg).astype(BF16).astype(F32)
    mine = ((iota((8, NLAT), 1) >> 2) & 7) == iota((8, NLAT), 0)
    spread = jnp.concatenate([jnp.where(mine, four[q : q + 1], 0.0) for q in range(8)], 0)
    moved = dot(spread.astype(BF16), select)
    return jnp.where(iota((YX, 128), 1) < 64, moved[:YX], moved[YX:])


def legendre_out(got, weight, leg, wave, select):
    low = iota((YX, 128), 1) < 64
    spread = jnp.concatenate([jnp.where(low, got, 0.0), jnp.where(low, 0.0, got)], 0)
    moved = dot(spread.astype(BF16), select, ((1,), (1,)))
    mine = ((iota((8, NLAT), 1) >> 2) & 7) == iota((8, NLAT), 0)
    rows = [
        jnp.sum(jnp.where(mine, moved[q * 8 : (q + 1) * 8], 0.0), 0, keepdims=True) for q in range(8)
    ]
    weighted = (jnp.concatenate(rows, 0) * weight).astype(BF16)
    result = dot(weighted, leg, ((1,), (1,)))
    result = jnp.where(iota(result.shape, 1) >= wave, result, 0.0)
    return result[:4], result[4:]


def turn(got):
    flipped = jnp.concatenate([got] * 4, 0).T
    group = iota((32, 128), 1) >> 5
    out = flipped[:32]
    for q in range(1, 4):
        out = jnp.where(group == q, flipped[q * 32 : (q + 1) * 32], out)
    return out


def roll(x, shift, axis):
    return pltpu.roll(x, shift % x.shape[axis], axis)


def swap_fours(x):
    line = iota(x.shape, 0) & 3
    group = iota(x.shape, 1) >> 5
    out = x
    for d in range(1, 4):
        moved = roll(x, -32 * d, 1)
        out = jnp.where(line - group == d, roll(moved, d, 0), out)
        out = jnp.where(line - group == d - 4, roll(moved, d - 4, 0), out)
    return out


def slot_selector():
    k = iota((192, 128), 0) & 62
    lane = iota((192, 128), 1)
    return one_hot(k == ((lane >> 5) * 16 + (lane & 7) * 2))


def slot_order(waves, pick):
    both = jnp.concatenate([(waves >> 3).astype(F32), (waves & 7).astype(F32)], 0)
    k = iota((8, 192), 1)
    part = (k >> 6) + (k & 1) * 3
    spread = jnp.concatenate([jnp.where(part == q, both, 0.0) for q in range(6)], 0)
    moved = dot(spread.astype(BF16), pick)
    row = iota((8, 128), 0)
    scale = jnp.where((row & 3) == ((iota((8, 128), 1) >> 3) & 3), jnp.where(row < 4, 8.0, 1.0), 0.0)
    return jnp.concatenate(
        [jnp.sum(moved[q * 8 : (q + 1) * 8] * scale, 0, keepdims=True) for q in range(6)], 1
    )


SIN_TERMS = [(-1.0) ** n * math.pi ** (2 * n + 1) / math.factorial(2 * n + 1) for n in range(7)]
COS_TERMS = [(-1.0) ** n * math.pi ** (2 * n) / math.factorial(2 * n) for n in range(8)]


def circle(points, waves, length):
    product = points * waves
    inverse = 1.0 / length
    rest = product - jnp.floor(product * inverse + 0.5) * length
    turn = rest * inverse
    square = turn * turn
    sine = jnp.full_like(square, SIN_TERMS[-1])
    for term in SIN_TERMS[-2::-1]:
        sine = sine * square + term
    sine = sine * turn
    cosine = jnp.full_like(square, COS_TERMS[-1])
    for term in COS_TERMS[-2::-1]:
        cosine = cosine * square + term
    return 1.0 - 2.0 * sine * sine, 2.0 * sine * cosine


def split(x):
    high = x.astype(BF16)
    return high, (x - high.astype(F32)).astype(BF16)


def tables(waves, length):
    row = iota((48, SLOTS), 0)
    points = jnp.where(row < NA_PAD, row * NB, jnp.where(row < 40, (row - NA_PAD) * 8, row - 40))
    cosine, sine = circle(points.astype(F32), waves, length)
    parts = []
    for lanes in PARTS:
        parts += [cosine[:NA_PAD, lanes], sine[:NA_PAD, lanes]]
    high, low = split(jnp.concatenate(parts, 1))
    outer = jnp.concatenate([high.astype(F32), low.astype(F32)], 0).astype(BF16)
    return outer, cosine[NA_PAD:], sine[NA_PAD:]


def factors(waves, lengths):
    empty = waves >= float(M)
    rows = [jnp.where(empty, 0.0, jnp.where(waves == 0.0, 1.0, 2.0))]
    rows += [jnp.where(empty, 0.0, 1.0 / n) for n in lengths]
    rows += [jnp.broadcast_to(n, waves.shape) for n in lengths]
    return jnp.concatenate(rows + [jnp.zeros((3, SLOTS), F32)], 0)


def grid_rows(got, factor, outer, cosine, sine):
    got = swap_fours(got)
    raws = [jnp.zeros((NB, NT), F32) for _ in range(2)]
    for q, lanes in enumerate(PARTS):
        for r in range(2):
            wide = slice(q * 256, (q + 1) * 256)
            cos_one, sin_one = cosine[r, 16:, lanes], sine[r, 16:, lanes]
            real = got[q * 4 + r : q * 4 + r + 1] * factor[0:1, lanes]
            imag = got[q * 4 + 2 + r : q * 4 + 3 + r] * factor[0:1, lanes]
            start_real = real * cos_one - imag * sin_one
            start_imag = real * sin_one + imag * cos_one
            mixed = []
            for j in range(16):
                c, s = cosine[r, j : j + 1, lanes], sine[r, j : j + 1, lanes]
                mixed.append(
                    jnp.concatenate([start_real * c - start_imag * s, -(start_real * s + start_imag * c)], 1)
                )
            high = jnp.concatenate(mixed, 0).astype(BF16)
            raws[r] = raws[r] + dot(high, outer[r, :, wide], ((1,), (1,)))
    grids, flips = [], []
    for r in range(2):
        raw = raws[r].T
        raw = raw[:NA_PAD] + raw[NA_PAD:]
        shaped = raw * (1.0 + 0.5 * jnp.tanh(raw))
        point = iota((NA_PAD, NB), 0) * NB + iota((NA_PAD, NB), 1)
        shaped = jnp.where(point.astype(F32) < factor[3 + r : 4 + r, :NB], shaped, 0.0)
        rounded = shaped.astype(BF16).astype(F32)
        grids.append(rounded)
        flips.append(jnp.concatenate([rounded, rounded], 0).T.astype(BF16))
    lines = [None] * 24
    for q, lanes in enumerate(PARTS):
        for r in range(2):
            wide = slice(q * 256, (q + 1) * 256)
            back = dot(flips[r], outer[r, :, wide])
            total_cos = jnp.zeros((8, 128), F32)
            total_sin = jnp.zeros((8, 128), F32)
            for j in range(16):
                c, s = cosine[r, j : j + 1, lanes], sine[r, j : j + 1, lanes]
                rows = slice(j * 8, (j + 1) * 8)
                back_cos, back_sin = back[rows, :128], back[rows, 128:]
                total_cos = total_cos + (back_cos * c - back_sin * s)
                total_sin = total_sin + (back_cos * s + back_sin * c)
            cos_one, sin_one = cosine[r, 16:, lanes], sine[r, 16:, lanes]
            part = factor[1 + r : 2 + r, lanes]
            lines[q * 4 + r] = jnp.sum(total_cos * cos_one - total_sin * sin_one, 0, keepdims=True) * part
            lines[q * 4 + 2 + r] = jnp.sum(total_cos * sin_one + total_sin * cos_one, 0, keepdims=True) * -part
    back = swap_fours(jnp.concatenate(lines, 0))
    return grids[0], grids[1], back.astype(BF16).astype(F32)


def select_kernel(pick_ref, select_ref):
    pick_ref[...] = slot_selector()
    select_ref[...] = row_selector()


def start_kernel(
    waves_ref, length_ref, weight_ref, pick_ref, select_ref, spec_ref, leg_ref,
    out_ref, wave_ref, line_ref, factor_ref, outer_ref, cos_ref, sin_ref,
):
    waves = waves_ref[...]
    length = length_ref[...].reshape(1, 2)
    lat_index = (lax.axis_index("z") * 8 + lax.axis_index("y")) * 2 + lax.axis_index("c")
    here = (iota((4, 192), 0) == lax.axis_index("x")) & (iota((4, 192), 1) == lat_index)
    own = jnp.where(here, waves.astype(F32), 0.0)
    own = jnp.sum(jnp.sum(own, 0, keepdims=True), 1, keepdims=True)
    wave_ref[...] = jnp.broadcast_to(own, (1, 128))
    line_ref[...] = weight_ref[...].reshape(1, NLAT)
    order = slot_order(waves, pick_ref[...])
    lengths = [length[:, r : r + 1].astype(F32) for r in range(2)]
    factor_ref[...] = factors(order, lengths)
    for r in range(2):
        outer_ref[r], cos_ref[r], sin_ref[r] = tables(order, lengths[r])
    out = legendre_in(spec_ref[0, 0], leg_ref[0, 0], own.astype(jnp.int32), select_ref[...])
    out_ref[...] = out.reshape(YX, 1, 128)


def turn_in_kernel(got_ref, out_ref):
    out_ref[...] = turn(got_ref[...].reshape(YX, 128))[:ZC].reshape(ZC, 1, 128)


def grid_kernel(got_ref, factor_ref, outer_ref, cos_ref, sin_ref, rows_ref, out_ref):
    one, two, out = grid_rows(
        got_ref[...].reshape(ZC, 128), factor_ref, outer_ref, cos_ref, sin_ref
    )
    rows_ref[0] = one
    rows_ref[1] = two
    out_ref[...] = out.reshape(ZC, 1, 128)


def turn_out_kernel(got_ref, out_ref):
    got = jnp.concatenate([got_ref[...].reshape(ZC, 128), jnp.zeros((YX - ZC, 128), F32)], 0)
    out_ref[...] = turn(got).reshape(YX, 1, 128)


def legendre_out_kernel(wave_ref, select_ref, weight_ref, got_ref, leg_ref, rows_ref, out_ref, grid_ref):
    for a in range(NA):
        grid_ref[0, :, a * NB : (a + 1) * NB] = rows_ref[:, a, :].astype(BF16)
    wave = wave_ref[:, :1].astype(jnp.int32)
    real, imag = legendre_out(got_ref[...].reshape(YX, 128), weight_ref[...], leg_ref[0, 0], wave, select_ref[...])
    out_ref[0, 0, :, :NDEG] = real.astype(BF16)
    out_ref[0, 0, :, NDEG:] = imag.astype(BF16)


VMEM = pl.BlockSpec(memory_space=pltpu.VMEM)
SMEM = pl.BlockSpec(memory_space=pltpu.SMEM)


def call(kernel, name, in_specs, outs, flops=10**6):
    single = not isinstance(outs, list)
    return pl.pallas_call(
        kernel,
        name=name,
        in_specs=in_specs,
        out_specs=VMEM if single else [VMEM] * len(outs),
        out_shape=outs if single else tuple(outs),
        compiler_params=pltpu.CompilerParams(vmem_limit_bytes=24 * 1024 * 1024),
        cost_estimate=pl.CostEstimate(flops=flops, bytes_accessed=100000, transcendentals=0),
    )


def shape(*dims, dtype=F32):
    return jax.ShapeDtypeStruct(dims, dtype)


def shards(spectral_in, legendre, slot_wave, row_length, quad_weight):
    pick, select = call(
        select_kernel, "select", [], [shape(192, 128, dtype=BF16), shape(NLAT, 128, dtype=BF16)], 2 * 10**9
    )()
    to_send, wave, weight, factor, outer, cosine, sine = call(
        start_kernel,
        "start",
        [VMEM] * 7,
        [
            shape(YX, 1, 128),
            shape(1, 128),
            shape(1, NLAT),
            shape(8, SLOTS),
            shape(2, 2 * NA_PAD, 2 * SLOTS, dtype=BF16),
            shape(2, 24, SLOTS),
            shape(2, 24, SLOTS),
        ],
    )(slot_wave, row_length, quad_weight, pick, select, spectral_in, legendre)
    got = lax.all_to_all(to_send, ("x", "y"), 0, 0, tiled=True)
    to_send = call(turn_in_kernel, "turn_in", [VMEM], shape(ZC, 1, 128))(got)
    got = lax.all_to_all(to_send, ("c", "z"), 0, 0, tiled=True)
    rows, to_send = call(
        grid_kernel, "grid", [VMEM] * 5, [shape(2, NA_PAD, NB), shape(ZC, 1, 128)]
    )(got, factor, outer, cosine, sine)
    got = lax.all_to_all(to_send, ("c", "z"), 0, 0, tiled=True)
    to_send = call(turn_out_kernel, "turn_out", [VMEM], shape(YX, 1, 128))(got)
    got = lax.all_to_all(to_send, ("x", "y"), 0, 0, tiled=True)
    spectral_out, grid_field = call(
        legendre_out_kernel,
        "legendre_out",
        [VMEM] * 6,
        [shape(1, 1, 4, 2 * NDEG, dtype=BF16), shape(1, 2, NLON, dtype=BF16)],
    )(wave, select, weight, got, legendre, rows)
    return grid_field, spectral_out


def solution(mesh):
    cut = Mesh(mesh.devices.reshape(12, 8, 2, 4), ("z", "y", "c", "x"))
    lat = ("z", "y", "c")
    in_specs = (P("x", lat, None, None), P("x", lat, None, None), P(), P(lat), P())
    out_specs = (P("x", lat, None), P("x", lat, None, None))
    return jax.shard_map(shards, mesh=cut, in_specs=in_specs, out_specs=out_specs, check_vma=False)
```

```python
import math

import jax
import jax.numpy as jnp
from jax import lax
from jax.experimental import pallas as pl
from jax.experimental.pallas import tpu as pltpu
from jax.sharding import Mesh
from jax.sharding import PartitionSpec as P

M = 640
NDEG = 640
NLAT = 384
NLON = 2688
SLOTS = 768
ZC = 24
YX = 32
NB = 128
NA = 21
NA_PAD = 24
NT = 24

PARTS = [slice(q * 128, (q + 1) * 128) for q in range(6)]

F32 = jnp.float32
BF16 = jnp.bfloat16


def iota(shape, dim):
    return lax.broadcasted_iota(jnp.int32, shape, dim)


def dot(x, y, dims=((1,), (0,))):
    return lax.dot_general(x, y, (dims, ((), ())), preferred_element_type=F32)


def one_hot(cond):
    return jnp.where(cond, 1.0, 0.0).astype(BF16)


def row_selector():
    l = iota((NLAT, 128), 0)
    lane = iota((NLAT, 128), 1)
    return one_hot((lane & 63) == ((l & 1) * 32 + ((l >> 1) & 1) * 12 + (l >> 5)))


def legendre_in(spec, leg, wave, select):
    both = jnp.concatenate([spec[:, :NDEG].astype(F32), spec[:, NDEG:].astype(F32)], 0)
    kept = jnp.where(iota(both.shape, 1) >= wave, both, 0.0).astype(BF16)
    four = dot(kept, leg).astype(BF16).astype(F32)
    mine = ((iota((8, NLAT), 1) >> 2) & 7) == iota((8, NLAT), 0)
    spread = jnp.concatenate([jnp.where(mine, four[q : q + 1], 0.0) for q in range(8)], 0)
    moved = dot(spread.astype(BF16), select)
    return jnp.where(iota((YX, 128), 1) < 64, moved[:YX], moved[YX:])


def legendre_out(got, weight, leg, wave, select):
    low = iota((YX, 128), 1) < 64
    spread = jnp.concatenate([jnp.where(low, got, 0.0), jnp.where(low, 0.0, got)], 0)
    moved = dot(spread.astype(BF16), select, ((1,), (1,)))
    mine = ((iota((8, NLAT), 1) >> 2) & 7) == iota((8, NLAT), 0)
    rows = [
        jnp.sum(jnp.where(mine, moved[q * 8 : (q + 1) * 8], 0.0), 0, keepdims=True) for q in range(8)
    ]
    weighted = (jnp.concatenate(rows, 0) * weight).astype(BF16)
    result = dot(weighted, leg, ((1,), (1,)))
    result = jnp.where(iota(result.shape, 1) >= wave, result, 0.0)
    return result[:4], result[4:]


def turn(got):
    flipped = jnp.concatenate([got] * 4, 0).T
    group = iota((32, 128), 1) >> 5
    out = flipped[:32]
    for q in range(1, 4):
        out = jnp.where(group == q, flipped[q * 32 : (q + 1) * 32], out)
    return out


def roll(x, shift, axis):
    return pltpu.roll(x, shift % x.shape[axis], axis)


def swap_fours(x):
    line = iota(x.shape, 0) & 3
    group = iota(x.shape, 1) >> 5
    out = x
    for d in range(1, 4):
        moved = roll(x, -32 * d, 1)
        out = jnp.where(line - group == d, roll(moved, d, 0), out)
        out = jnp.where(line - group == d - 4, roll(moved, d - 4, 0), out)
    return out


def slot_selector():
    k = iota((192, 128), 0) & 62
    lane = iota((192, 128), 1)
    return one_hot(k == ((lane >> 5) * 16 + (lane & 7) * 2))


def slot_order(waves, pick):
    both = jnp.concatenate([(waves >> 3).astype(F32), (waves & 7).astype(F32)], 0)
    k = iota((8, 192), 1)
    part = (k >> 6) + (k & 1) * 3
    spread = jnp.concatenate([jnp.where(part == q, both, 0.0) for q in range(6)], 0)
    moved = dot(spread.astype(BF16), pick)
    row = iota((8, 128), 0)
    scale = jnp.where((row & 3) == ((iota((8, 128), 1) >> 3) & 3), jnp.where(row < 4, 8.0, 1.0), 0.0)
    return jnp.concatenate(
        [jnp.sum(moved[q * 8 : (q + 1) * 8] * scale, 0, keepdims=True) for q in range(6)], 1
    )


SIN_TERMS = [(-1.0) ** n * math.pi ** (2 * n + 1) / math.factorial(2 * n + 1) for n in range(7)]
COS_TERMS = [(-1.0) ** n * math.pi ** (2 * n) / math.factorial(2 * n) for n in range(8)]


def circle(points, waves, length):
    product = points * waves
    inverse = 1.0 / length
    rest = product - jnp.floor(product * inverse + 0.5) * length
    turn = rest * inverse
    square = turn * turn
    sine = jnp.full_like(square, SIN_TERMS[-1])
    for term in SIN_TERMS[-2::-1]:
        sine = sine * square + term
    sine = sine * turn
    cosine = jnp.full_like(square, COS_TERMS[-1])
    for term in COS_TERMS[-2::-1]:
        cosine = cosine * square + term
    return 1.0 - 2.0 * sine * sine, 2.0 * sine * cosine


def split(x):
    high = x.astype(BF16)
    return high, (x - high.astype(F32)).astype(BF16)


def tables(waves, length):
    row = iota((48, SLOTS), 0)
    points = jnp.where(row < NA_PAD, row * NB, jnp.where(row < 40, (row - NA_PAD) * 8, row - 40))
    cosine, sine = circle(points.astype(F32), waves, length)
    parts = []
    for lanes in PARTS:
        parts += [cosine[:NA_PAD, lanes], sine[:NA_PAD, lanes]]
    outer = jnp.concatenate(parts, 1).astype(BF16)
    return outer, cosine[NA_PAD:], sine[NA_PAD:]


def factors(waves, lengths):
    empty = waves >= float(M)
    rows = [jnp.where(empty, 0.0, jnp.where(waves == 0.0, 1.0, 2.0))]
    rows += [jnp.where(empty, 0.0, 1.0 / n) for n in lengths]
    rows += [jnp.broadcast_to(n, waves.shape) for n in lengths]
    return jnp.concatenate(rows + [jnp.zeros((3, SLOTS), F32)], 0)


def grid_rows(got, factor, outer, cosine, sine, mix_ref):
    got = swap_fours(got)
    for q, lanes in enumerate(PARTS):
        for r in range(2):
            wide = slice(q * 256, (q + 1) * 256)
            cos_one, sin_one = cosine[r, 16:, lanes], sine[r, 16:, lanes]
            real = got[q * 4 + r : q * 4 + r + 1] * factor[0:1, lanes]
            imag = got[q * 4 + 2 + r : q * 4 + 3 + r] * factor[0:1, lanes]
            start_real = real * cos_one - imag * sin_one
            start_imag = real * sin_one + imag * cos_one
            mixed = []
            for j in range(16):
                c, s = cosine[r, j : j + 1, lanes], sine[r, j : j + 1, lanes]
                mixed.append(
                    jnp.concatenate([start_real * c - start_imag * s, -(start_real * s + start_imag * c)], 1)
                )
            mix_ref[r, :, wide] = jnp.concatenate(mixed, 0).astype(BF16)
    grids, flips = [], []
    for r in range(2):
        raw = dot(outer[r], mix_ref[r], ((1,), (1,)))
        shaped = raw * (1.0 + 0.5 * jnp.tanh(raw))
        point = iota((NA_PAD, NB), 0) * NB + iota((NA_PAD, NB), 1)
        shaped = jnp.where(point.astype(F32) < factor[3 + r : 4 + r, :NB], shaped, 0.0)
        rounded = shaped.astype(BF16).astype(F32)
        grids.append(rounded)
        flips.append(rounded.T.astype(BF16))
    lines = [None] * 24
    for q, lanes in enumerate(PARTS):
        for r in range(2):
            wide = slice(q * 256, (q + 1) * 256)
            back = dot(flips[r], outer[r, :, wide])
            total_cos = jnp.zeros((8, 128), F32)
            total_sin = jnp.zeros((8, 128), F32)
            for j in range(16):
                c, s = cosine[r, j : j + 1, lanes], sine[r, j : j + 1, lanes]
                rows = slice(j * 8, (j + 1) * 8)
                back_cos, back_sin = back[rows, :128], back[rows, 128:]
                total_cos = total_cos + (back_cos * c - back_sin * s)
                total_sin = total_sin + (back_cos * s + back_sin * c)
            cos_one, sin_one = cosine[r, 16:, lanes], sine[r, 16:, lanes]
            part = factor[1 + r : 2 + r, lanes]
            lines[q * 4 + r] = jnp.sum(total_cos * cos_one - total_sin * sin_one, 0, keepdims=True) * part
            lines[q * 4 + 2 + r] = jnp.sum(total_cos * sin_one + total_sin * cos_one, 0, keepdims=True) * -part
    back = swap_fours(jnp.concatenate(lines, 0))
    return grids[0], grids[1], back.astype(BF16).astype(F32)


def select_kernel(pick_ref, select_ref):
    pick_ref[...] = slot_selector()
    select_ref[...] = row_selector()


def start_kernel(
    waves_ref, length_ref, weight_ref, pick_ref, select_ref, spec_ref, leg_ref,
    out_ref, wave_ref, line_ref, factor_ref, outer_ref, cos_ref, sin_ref,
):
    waves = waves_ref[...]
    length = length_ref[...].reshape(1, 2)
    lat_index = (lax.axis_index("z") * 8 + lax.axis_index("y")) * 2 + lax.axis_index("c")
    here = (iota((4, 192), 0) == lax.axis_index("x")) & (iota((4, 192), 1) == lat_index)
    own = jnp.where(here, waves.astype(F32), 0.0)
    own = jnp.sum(jnp.sum(own, 0, keepdims=True), 1, keepdims=True)
    wave_ref[...] = jnp.broadcast_to(own, (1, 128))
    line_ref[...] = weight_ref[...].reshape(1, NLAT)
    order = slot_order(waves, pick_ref[...])
    lengths = [length[:, r : r + 1].astype(F32) for r in range(2)]
    factor_ref[...] = factors(order, lengths)
    for r in range(2):
        outer_ref[r], cos_ref[r], sin_ref[r] = tables(order, lengths[r])
    out = legendre_in(spec_ref[0, 0], leg_ref[0, 0], own.astype(jnp.int32), select_ref[...])
    out_ref[...] = out.reshape(YX, 1, 128)


def turn_in_kernel(got_ref, out_ref):
    out_ref[...] = turn(got_ref[...].reshape(YX, 128))[:ZC].reshape(ZC, 1, 128)


def grid_kernel(got_ref, factor_ref, outer_ref, cos_ref, sin_ref, rows_ref, out_ref, mix_ref):
    one, two, out = grid_rows(
        got_ref[...].reshape(ZC, 128), factor_ref, outer_ref, cos_ref, sin_ref, mix_ref
    )
    rows_ref[0] = one
    rows_ref[1] = two
    out_ref[...] = out.reshape(ZC, 1, 128)


def turn_out_kernel(got_ref, out_ref):
    got = jnp.concatenate([got_ref[...].reshape(ZC, 128), jnp.zeros((YX - ZC, 128), F32)], 0)
    out_ref[...] = turn(got).reshape(YX, 1, 128)


def legendre_out_kernel(wave_ref, select_ref, weight_ref, got_ref, leg_ref, rows_ref, out_ref, grid_ref):
    wave = wave_ref[:, :1].astype(jnp.int32)
    real, imag = legendre_out(got_ref[...].reshape(YX, 128), weight_ref[...], leg_ref[0, 0], wave, select_ref[...])
    out_ref[0, 0, :, :NDEG] = real.astype(BF16)
    out_ref[0, 0, :, NDEG:] = imag.astype(BF16)
    for a in range(NA):
        grid_ref[0, :, a * NB : (a + 1) * NB] = rows_ref[:, a, :].astype(BF16)


VMEM = pl.BlockSpec(memory_space=pltpu.VMEM)
SMEM = pl.BlockSpec(memory_space=pltpu.SMEM)


def call(kernel, name, in_specs, outs, flops=10**6, scratch=()):
    single = not isinstance(outs, list)
    return pl.pallas_call(
        kernel,
        name=name,
        in_specs=in_specs,
        out_specs=VMEM if single else [VMEM] * len(outs),
        out_shape=outs if single else tuple(outs),
        scratch_shapes=scratch,
        compiler_params=pltpu.CompilerParams(vmem_limit_bytes=24 * 1024 * 1024),
        cost_estimate=pl.CostEstimate(flops=flops, bytes_accessed=100000, transcendentals=0),
    )


def shape(*dims, dtype=F32):
    return jax.ShapeDtypeStruct(dims, dtype)


def shards(spectral_in, legendre, slot_wave, row_length, quad_weight):
    pick, select = call(
        select_kernel, "select", [], [shape(192, 128, dtype=BF16), shape(NLAT, 128, dtype=BF16)], 2 * 10**9
    )()
    to_send, wave, weight, factor, outer, cosine, sine = call(
        start_kernel,
        "start",
        [VMEM] * 7,
        [
            shape(YX, 1, 128),
            shape(1, 128),
            shape(1, NLAT),
            shape(8, SLOTS),
            shape(2, NT, 2 * SLOTS, dtype=BF16),
            shape(2, 24, SLOTS),
            shape(2, 24, SLOTS),
        ],
    )(slot_wave, row_length, quad_weight, pick, select, spectral_in, legendre)
    got = lax.all_to_all(to_send, ("x", "y"), 0, 0, tiled=True)
    to_send = call(turn_in_kernel, "turn_in", [VMEM], shape(ZC, 1, 128))(got)
    got = lax.all_to_all(to_send, ("c", "z"), 0, 0, tiled=True)
    rows, to_send = call(
        grid_kernel,
        "grid",
        [VMEM] * 5,
        [shape(2, NA_PAD, NB), shape(ZC, 1, 128)],
        scratch=[pltpu.VMEM((2, NB, 2 * SLOTS), BF16)],
    )(got, factor, outer, cosine, sine)
    got = lax.all_to_all(to_send, ("c", "z"), 0, 0, tiled=True)
    to_send = call(turn_out_kernel, "turn_out", [VMEM], shape(YX, 1, 128))(got)
    got = lax.all_to_all(to_send, ("x", "y"), 0, 0, tiled=True)
    spectral_out, grid_field = call(
        legendre_out_kernel,
        "legendre_out",
        [VMEM] * 6,
        [shape(1, 1, 4, 2 * NDEG, dtype=BF16), shape(1, 2, NLON, dtype=BF16)],
    )(wave, select, weight, got, legendre, rows)
    return grid_field, spectral_out


def solution(mesh):
    cut = Mesh(mesh.devices.reshape(12, 8, 2, 4), ("z", "y", "c", "x"))
    lat = ("z", "y", "c")
    in_specs = (P("x", lat, None, None), P("x", lat, None, None), P(), P(lat), P())
    out_specs = (P("x", lat, None), P("x", lat, None, None))
    return jax.shard_map(shards, mesh=cut, in_specs=in_specs, out_specs=out_specs, check_vma=False)
```
